32 devices in a mesh: sec: 2 (over core), tile: 16 (over z, y, x).
Axes of the slice: x: 2, y: 2, z: 4, core: 2. Of those that a mesh axis runs over, the one named last changes fastest.
Arguments:
- adjoint_state: bfloat16 [2, 75, 589824], P('sec', None, 'tile'), may hold values from -6 to 6
- tangent_coef: bfloat16 [2, 75, 589824], P('sec', None, 'tile'), may hold values from 0.5 to 1.5
- column_ops: bfloat16 [2, 16, 75, 75], P('sec')
- surf_read: bfloat16 [2, 4, 75], P('sec'), may hold values from -0.75 to 0.75
- surf_write: float32 [2, 75, 4], P('sec'), may hold values from -3 to 3
- remap_weights: bfloat16 [16, 16, 16, 4096], P('tile')
- pair_atmos: int32 [16, 16, 16], P('tile'), may hold values from 0 to 575
- pair_ocean: int32 [16, 16, 16], P('tile'), may hold values from 0 to 9215, as said below
- list_len: int32 [16, 16], P('tile'), may hold values from 0 to 16, as said below
- ocean_owned: int32 [16, 576], P('tile'), may hold values from 0 to 9215, as said below
Outputs:
- adjoint_out: bfloat16 [2, 75, 589824], P('sec', None, 'tile')
The draws below stay inside these ranges and needn't reach their ends.
Inputs may be any that keep to these rules, and one draw needn't show every extreme that they name: pair_ocean[t, d, c] is one of the blocks in row d of ocean_owned. Every global ocean block stands exactly once in ocean_owned. Slots c >= list_len[t, d] are empty; in every draw some ocean tile receives a full list of 16 pairs from every atmosphere tile.
All inputs are finite; a program needn't handle non-finite values.
Results may differ from the reference program's by a relative error of at most 0.012.
Values may be sent and summed in bfloat16 or wider, within the bound.
A program may use at most 128 MiB of HBM per device.

```python
import jax
import jax.numpy as jnp
from jax import lax

LEV = 75
NF = 4
BLK = 64
CAP = 16
NSTEP = 16
CELL_DEV = 36864
TILES = 16
BLOCKS_DEV = 576
CELLS = 589824


def ownership(key):
    order = jax.random.permutation(jax.random.fold_in(key, 11), TILES * BLOCKS_DEV)
    return order.astype(jnp.int32).reshape(TILES, BLOCKS_DEV)


def draw_ocean_owned(key, part):
    return ownership(key)


def draw_pair_ocean(key, part):
    owned = ownership(key)
    chosen = jax.random.randint(jax.random.fold_in(key, 12), (TILES, TILES, CAP), 0, BLOCKS_DEV)
    tile_index = jnp.arange(TILES, dtype=jnp.int32)[None, :, None]
    return owned[tile_index, chosen].astype(jnp.int32)


def draw_list_len(key, part):
    lengths = jax.random.randint(jax.random.fold_in(key, 21), (TILES, TILES), 0, CAP + 1)
    full_tile = jax.random.randint(jax.random.fold_in(key, 22), (), 0, TILES)
    tile_index = jnp.arange(TILES, dtype=jnp.int32)
    return jnp.where(tile_index[None, :] == full_tile, CAP, lengths).astype(jnp.int32)


def draw_column_ops(key, part):
    noise_part = jax.random.normal(jax.random.fold_in(key, 31), (2, NSTEP, LEV, LEV), jnp.float32)
    level_index = jnp.arange(LEV)
    identity = (level_index[:, None] == level_index[None, :]).astype(jnp.float32)
    return (0.9 * identity + 0.35 * LEV ** (-0.5) * noise_part).astype(jnp.bfloat16)


def draw_remap_weights(key, part):
    spread_part = jax.random.uniform(jax.random.fold_in(key, 41), (TILES, TILES, CAP, BLK, BLK), jnp.float32, 0.0, 2.0 / BLK)
    cell_index = jnp.arange(BLK)
    identity = (cell_index[:, None] == cell_index[None, :]).astype(jnp.float32)
    weights = 0.5 * identity + spread_part * (1.0 - identity)
    return weights.reshape(TILES, TILES, CAP, BLK * BLK).astype(jnp.bfloat16)


def plant(drawn, own_key, least, top_value):
    longest = drawn.shape.index(max(drawn.shape))
    spots = []
    for shift in (0, 1):
        where = [jax.random.randint(jax.random.fold_in(own_key, axis), (), 0, length) for axis, length in enumerate(drawn.shape)]
        where[longest] = (where[longest] + shift) % drawn.shape[longest]
        spots.append(tuple(where))
    return drawn.at[spots[0]].set(least).at[spots[1]].set(top_value)


def levels(own_key, extent, shards, least, top_value):
    loudness = 1.0
    for position, shards_of in shards:
        heights = jax.random.uniform(jax.random.fold_in(jax.random.fold_in(own_key, 6), position), (shards_of,), jnp.float32, least / len(shards), top_value / len(shards))
        loudness = loudness * jnp.repeat(jnp.exp(heights), extent[position] // shards_of).reshape((-1,) + (1,) * (len(extent) - 1 - position))
    return loudness


def noise(key, extent, deviation, limit, shards=(), kind=jnp.bfloat16):
    entries = jax.random.normal(key, extent, jnp.float32) * deviation
    if len(shards) > 0:
        entries = levels(key, extent, shards, -0.22, 0.18) * entries
    return jnp.clip(entries, min=-limit, max=limit).astype(kind)


def setup_inputs(seed: int = 0) -> dict:
    seeds = jax.random.split(jax.random.key(seed), 11)
    adjoint_state = noise(seeds[0], (2, LEV, CELLS), 1.0, 6.0, ((0, 2), (2, 16)))
    tangent_coef = jnp.clip(1.0 + 0.1 * jax.random.normal(seeds[1], (2, LEV, CELLS), jnp.float32), 0.5, 1.5).astype(jnp.bfloat16)
    column_ops = draw_column_ops(jax.random.fold_in(seeds[10], 71), 0)
    surf_read = noise(seeds[3], (2, NF, LEV), LEV ** -0.5, 0.75, ((0, 2),))
    surf_write = noise(seeds[4], (2, LEV, NF), NF ** -0.5, 3.0, ((0, 2),), jnp.float32)
    remap_weights = draw_remap_weights(jax.random.fold_in(seeds[10], 71), 0)
    pair_atmos = plant(jax.random.randint(seeds[6], (TILES, TILES, CAP), 0, BLOCKS_DEV), jax.random.fold_in(seeds[6], 1), 0, BLOCKS_DEV - 1).astype(jnp.int32)
    pair_ocean = draw_pair_ocean(jax.random.fold_in(seeds[10], 71), 0)
    list_len = draw_list_len(jax.random.fold_in(seeds[10], 71), 0)
    ocean_owned = draw_ocean_owned(jax.random.fold_in(seeds[10], 71), 0)
    return dict(adjoint_state=adjoint_state, tangent_coef=tangent_coef, column_ops=column_ops, surf_read=surf_read, surf_write=surf_write, remap_weights=remap_weights, pair_atmos=pair_atmos, pair_ocean=pair_ocean, list_len=list_len, ocean_owned=ocean_owned)


def sweep_section(state_part, coef_part, ops_part):
    columns = state_part.reshape(LEV, TILES, CELL_DEV).transpose(1, 0, 2)
    factors = coef_part.reshape(LEV, TILES, CELL_DEV).transpose(1, 0, 2)

    def one_tile(packed):
        column, factor = packed

        def advance(current, operator):
            stepped = jnp.dot(operator.T, current, preferred_element_type=jnp.float32)
            return (stepped * factor).astype(jnp.bfloat16), None

        return lax.scan(advance, column, ops_part)[0]

    result = lax.map(one_tile, (columns, factors))
    return result.transpose(1, 0, 2).reshape(LEV, CELLS)


def reference(adjoint_state, tangent_coef, column_ops, surf_read, surf_write, remap_weights, pair_atmos, pair_ocean, list_len, ocean_owned):
    blocks = BLOCKS_DEV
    slot_count = TILES * CAP
    swept_atmos = sweep_section(adjoint_state[0], tangent_coef[0], column_ops[0])
    swept_ocean = sweep_section(adjoint_state[1], tangent_coef[1], column_ops[1])
    surface_atmos = jnp.dot(surf_read[0], adjoint_state[0], preferred_element_type=jnp.float32).astype(jnp.bfloat16)
    surface_ocean = jnp.dot(surf_read[1], adjoint_state[1], preferred_element_type=jnp.float32).astype(jnp.bfloat16)
    atmos_blocks = surface_atmos.reshape(NF, TILES * blocks, BLK).transpose(1, 0, 2)
    ocean_blocks = surface_ocean.reshape(NF, TILES * blocks, BLK).transpose(1, 0, 2)
    position_of = jnp.zeros((TILES * blocks,), jnp.int32).at[ocean_owned.reshape(-1)].set(
        (jnp.arange(TILES * blocks, dtype=jnp.int32) % blocks).astype(jnp.int32))
    dest_tile = jnp.broadcast_to(jnp.arange(TILES, dtype=jnp.int32)[None, :, None], (TILES, TILES, CAP))
    ocean_seg = (dest_tile * blocks + position_of[pair_ocean]).astype(jnp.int32)
    source_tile = jnp.broadcast_to(jnp.arange(TILES, dtype=jnp.int32)[:, None, None], (TILES, TILES, CAP))
    atmos_seg = (source_tile * blocks + pair_atmos).astype(jnp.int32)
    live_mask = jnp.arange(CAP, dtype=jnp.int32)[None, None, :] < list_len[:, :, None]

    def per_source(packed):
        weights_t, atmos_t, ocean_t, live_t = packed
        weights = weights_t.reshape(slot_count, BLK, BLK).astype(jnp.float32)
        picked = atmos_blocks[atmos_t.reshape(-1)].astype(jnp.float32)
        flux = jnp.einsum("snj,sjm->snm", picked, weights)
        flux = jnp.where(live_t.reshape(slot_count, 1, 1), flux, 0.0)
        echoes = ocean_blocks[ocean_t.reshape(-1)].astype(jnp.float32)
        back = jnp.einsum("sjm,snm->snj", weights, echoes)
        back = jnp.where(live_t.reshape(slot_count, 1, 1), back, 0.0)
        return flux, back

    flux_terms, back_terms = lax.map(per_source, (remap_weights, atmos_seg, ocean_seg, live_mask))
    ocean_sum = jax.ops.segment_sum(flux_terms.reshape(-1, NF * BLK), ocean_seg.reshape(-1), num_segments=TILES * blocks)
    ocean_forcing = ocean_sum.reshape(TILES * blocks, NF, BLK).transpose(1, 0, 2).reshape(NF, CELLS)
    atmos_sum = jax.ops.segment_sum(back_terms.reshape(-1, NF * BLK), atmos_seg.reshape(-1), num_segments=TILES * blocks)
    atmos_forcing = atmos_sum.reshape(TILES * blocks, NF, BLK).transpose(1, 0, 2).reshape(NF, CELLS)
    out_atmos = swept_atmos.astype(jnp.float32) + jnp.dot(surf_write[0], atmos_forcing, precision=lax.Precision.HIGHEST)
    out_ocean = swept_ocean.astype(jnp.float32) + jnp.dot(surf_write[1], ocean_forcing, precision=lax.Precision.HIGHEST)
    return jnp.stack([out_atmos, out_ocean]).astype(jnp.bfloat16)
```

```python
import functools

import jax
import jax.numpy as jnp
from jax import lax
from jax.experimental import pallas as pl
from jax.experimental.pallas import tpu as pltpu
from jax.sharding import PartitionSpec as P

NF = 4
BLK = 64
NSTEP = 16


def shifted(value, axis, steps):
    count = lax.axis_size(axis)
    first, last = (max(0, -steps), min(count, count - steps))
    return lax.ppermute(value, axis, [(source, source + steps) for source in range(first, last)])


def locate_blocks(arrived_ids, owned_row, slot_count, blocks):
    matches = arrived_ids.reshape(slot_count)[:, None] == owned_row[None, :]
    return jnp.sum(
        jnp.where(matches, lax.broadcasted_iota(jnp.int32, (slot_count, blocks), 1), 0), axis=1
    )


def forward_remap(picked, paired_weights, slot_count):
    half = BLK // 2
    split_rows = picked.reshape(slot_count, NF, half, 2)
    even_rows = split_rows[:, :, :, 0]
    odd_rows = split_rows[:, :, :, 1]
    first = jnp.einsum(
        "snj,sjq->snq", even_rows, paired_weights, preferred_element_type=jnp.float32
    )
    second = jnp.einsum(
        "snj,sjq->snq", odd_rows, paired_weights, preferred_element_type=jnp.float32
    )
    return first[:, :, :BLK] + second[:, :, BLK:]


def backward_remap(echoes, paired_weights, slot_count):
    blank = jnp.zeros_like(echoes)
    lower = jnp.concatenate([echoes, blank], 2)
    upper = jnp.concatenate([blank, echoes], 2)
    even_cells = jnp.einsum(
        "sjq,snq->snj", paired_weights, lower, preferred_element_type=jnp.float32
    )
    odd_cells = jnp.einsum(
        "sjq,snq->snj", paired_weights, upper, preferred_element_type=jnp.float32
    )
    return jnp.stack([even_cells, odd_cells], 3).reshape(slot_count, NF, BLK)


MXU = 256


def round_up(value, unit):
    return -(-value // unit) * unit


def sweep_kernel(levels, group, units, state_ref, coef_ref, ops_ref, write_ref, forcing_ref, out_ref, big):
    steps, rows, _ = ops_ref.shape
    full = group * rows

    @pl.when(pl.program_id(0) == 0)
    def _():
        place_row = lax.broadcasted_iota(jnp.int32, (rows, full), 0)
        place_lane = lax.broadcasted_iota(jnp.int32, (rows, full), 1)
        tiler = (lax.rem(place_lane, rows) == place_row).astype(jnp.bfloat16)
        for step in range(steps):
            tiled = jnp.dot(ops_ref[step], tiler, preferred_element_type=jnp.float32)
            for part in range(group):
                inside = (place_lane >= part * rows) & (place_lane < (part + 1) * rows)
                big[step, part * rows : (part + 1) * rows, :] = jnp.where(inside, tiled, 0.0).astype(jnp.bfloat16)

    valid = lax.broadcasted_iota(jnp.int32, (rows, MXU), 0) < levels

    def columns(unit, part):
        return pl.ds((unit * group + part) * MXU, MXU)

    current, factors = [], []
    for unit in range(units):
        pieces = [
            jnp.where(valid, state_ref[0, :, columns(unit, part)].astype(jnp.float32), 0.0).astype(jnp.bfloat16)
            for part in range(group)
        ]
        current.append(jnp.concatenate(pieces, axis=0))
        pieces = [
            jnp.where(valid, coef_ref[0, :, columns(unit, part)].astype(jnp.float32), 0.0) for part in range(group)
        ]
        factors.append(jnp.concatenate(pieces, axis=0))
    for step in range(steps):
        operator = big[step]
        for unit in range(units):
            stepped = jnp.dot(operator, current[unit], preferred_element_type=jnp.float32)
            current[unit] = (stepped * factors[unit]).astype(jnp.bfloat16)

    write = write_ref[...]
    write_high = write.astype(jnp.bfloat16).astype(jnp.float32)
    write_parts = jnp.concatenate([write_high, write_high, write - write_high], axis=1).astype(jnp.bfloat16)
    for unit in range(units):
        for part in range(group):
            forcing = forcing_ref[:, columns(unit, part)]
            high = forcing.astype(jnp.bfloat16).astype(jnp.float32)
            parts = jnp.concatenate([high, forcing - high, high], axis=0).astype(jnp.bfloat16)
            added = jnp.dot(write_parts, parts, preferred_element_type=jnp.float32)
            swept = current[unit][part * rows : (part + 1) * rows].astype(jnp.float32)
            out_ref[0, :, columns(unit, part)] = (swept + added).astype(jnp.bfloat16)


def sweep(state, coef, column_ops, surf_write, forcing):
    _, levels, cells = state.shape
    steps = column_ops.shape[1]
    rows = round_up(levels, 16)
    group = max(1, MXU // rows)
    width = group * MXU
    units = max(count for count in (1, 2, 3, 4) if cells % (width * count) == 0)
    block = width * units
    flipped = jnp.swapaxes(column_ops[0], 1, 2)
    flipped = jnp.pad(flipped, ((0, 0), (0, rows - levels), (0, rows - levels)))
    write = jnp.pad(surf_write[0], ((0, rows - levels), (0, 0)))
    wide = pl.BlockSpec((1, rows, block), lambda i: (0, 0, i))
    return pl.pallas_call(
        functools.partial(sweep_kernel, levels, group, units),
        out_shape=jax.ShapeDtypeStruct(state.shape, jnp.bfloat16),
        grid=(cells // block,),
        in_specs=[
            wide,
            wide,
            pl.BlockSpec(flipped.shape, lambda i: (0, 0, 0)),
            pl.BlockSpec(write.shape, lambda i: (0, 0)),
            pl.BlockSpec((NF, block), lambda i: (0, i)),
        ],
        out_specs=wide,
        scratch_shapes=[pltpu.VMEM((steps, group * rows, group * rows), jnp.bfloat16)],
        compiler_params=pltpu.CompilerParams(
            dimension_semantics=("arbitrary",), vmem_limit_bytes=40 * 1024 * 1024
        ),
        name="sweep",
    )(state, coef, flipped, write, forcing)


def body(
    adjoint_state,
    tangent_coef,
    column_ops,
    surf_read,
    surf_write,
    remap_weights,
    pair_atmos,
    pair_ocean,
    list_len,
    ocean_owned,
):
    tile_count = lax.axis_size("tile")
    section = lax.axis_index("sec")
    slot_cap = pair_atmos.shape[2]
    slot_count = tile_count * slot_cap
    blocks = ocean_owned.shape[1]
    column = adjoint_state[0]
    surface = jnp.dot(surf_read[0], column, preferred_element_type=jnp.float32).astype(jnp.bfloat16)
    surface_blocks = surface.reshape(NF, blocks, BLK).transpose(1, 0, 2)
    ocean_rows = surface_blocks.reshape(blocks, NF * BLK)
    paired_weights = remap_weights[0].reshape(slot_count, BLK // 2, 2 * BLK)
    source = pair_atmos[0].reshape(slot_count)
    live_mask = (
        lax.broadcasted_iota(jnp.int32, (tile_count, slot_cap), 1) < list_len[0][:, None]
    ).reshape(slot_count, 1, 1)
    picked = surface_blocks[source]
    partial_flux = forward_remap(picked, paired_weights, slot_count)
    partial_flux = jnp.where(live_mask, partial_flux, 0.0).reshape(tile_count, slot_cap, NF * BLK)
    targets = pair_ocean[0]
    received, arrived_ids = (
        lax.all_to_all(partial_flux, "tile", split_axis=0, concat_axis=0, tiled=True),
        lax.all_to_all(targets, "tile", split_axis=0, concat_axis=0, tiled=True),
    )
    arriving = shifted(received, "sec", 1)
    position = locate_blocks(arrived_ids, ocean_owned[0], slot_count, blocks)
    replies = ocean_rows[position].reshape(tile_count, slot_cap, NF * BLK)
    crossed = shifted(replies, "sec", -1)
    returned = lax.all_to_all(crossed, "tile", split_axis=0, concat_axis=0, tiled=True)
    ocean_terms = jax.ops.segment_sum(
        arriving.reshape(slot_count, NF * BLK), position, num_segments=blocks
    )
    ocean_forcing = (
        ocean_terms.reshape(blocks, NF, BLK).transpose(1, 0, 2).reshape(NF, blocks * BLK)
    )
    echoes = returned.reshape(slot_count, NF, BLK)
    back_terms = backward_remap(echoes, paired_weights, slot_count)
    back_terms = jnp.where(live_mask, back_terms, 0.0).reshape(slot_count, NF * BLK)
    atmos_terms = jax.ops.segment_sum(back_terms, source, num_segments=blocks)
    atmos_forcing = (
        atmos_terms.reshape(blocks, NF, BLK).transpose(1, 0, 2).reshape(NF, blocks * BLK)
    )
    forcing = jnp.where(section == 0, atmos_forcing, ocean_forcing)
    return sweep(adjoint_state, tangent_coef, column_ops, surf_write, forcing)


def solution(mesh):
    in_specs = (
        P("sec", None, "tile"),
        P("sec", None, "tile"),
        P("sec", None, None, None),
        P("sec", None, None),
        P("sec", None, None),
        P("tile", None, None, None),
        P("tile", None, None),
        P("tile", None, None),
        P("tile", None),
        P("tile", None),
    )
    out_specs = P("sec", None, "tile")
    return jax.shard_map(body, mesh=mesh, in_specs=in_specs, out_specs=out_specs, check_vma=False)
```

```python
import functools

import jax
import jax.numpy as jnp
from jax import lax
from jax.experimental import pallas as pl
from jax.experimental.pallas import tpu as pltpu
from jax.sharding import PartitionSpec as P

NF = 4
BLK = 64
MXU = 256
MESH = pl.DeviceIdType.MESH
F32 = jnp.float32
BF16 = jnp.bfloat16


def round_up(value, unit):
    return -(-value // unit) * unit


def iota(shape, axis):
    return lax.broadcasted_iota(jnp.int32, shape, axis)


def dot(left, right, contract=((1,), (0,))):
    return lax.dot_general(left, right, (contract, ((), ())), preferred_element_type=F32)


def one_hot(condition):
    return jnp.where(condition, 1.0, 0.0).astype(BF16)


def slot_column(rows, cap):
    spread = jnp.concatenate([jnp.broadcast_to(row, (cap, row.shape[1])) for row in rows], axis=0)
    chosen = iota(spread.shape, 1) == lax.rem(iota(spread.shape, 0), cap)
    return jnp.sum(jnp.where(chosen, spread.astype(F32), 0.0), axis=1, keepdims=True)


def exchange_kernel(
    tiles, cap, surface_ref, weights_ref, atmos_ref, ocean_ref, len_ref, owned_ref, out_ref,
    ids_send, ids_recv, data_send, data_recv, expanded, summed, sems,
):
    section = lax.axis_index("sec")
    me = lax.axis_index("tile")
    other = 1 - section
    slots = tiles * cap
    blocks = surface_ref.shape[1]
    chunks = weights_ref.shape[1] // MXU
    per_chunk = MXU // BLK
    ids_out, ids_in, data_out, data_in = [sems.at[i] for i in range(4)]

    def peer(i):
        return lax.rem(me + i, tiles)

    barrier = pltpu.get_barrier_semaphore()

    @pl.loop(0, tiles)
    def _(i):
        pl.semaphore_signal(barrier, inc=1, device_id=(other, peer(i)), device_id_type=MESH)

    pl.semaphore_wait(barrier, tiles)

    def send(source, target, send_sem, recv_sem):
        @pl.loop(0, tiles)
        def _(i):
            pltpu.make_async_remote_copy(
                src_ref=source.at[peer(i)],
                dst_ref=target.at[me],
                send_sem=send_sem,
                recv_sem=recv_sem,
                device_id=(other, peer(i)),
                device_id_type=MESH,
            ).start()

    def wait_all(buffer, sem):
        pltpu.make_async_copy(buffer, buffer, sem).wait()

    def surface_rows():
        return jnp.concatenate([surface_ref[n] for n in range(NF)], axis=1)

    def emit(forcing):
        for n in range(NF):
            out_ref[n] = forcing[:, n * BLK : (n + 1) * BLK]

    @pl.when(section == 0)
    def _():
        for d in range(tiles):
            ids_send[d, 0:1, 0:cap] = ocean_ref[d : d + 1, :]
        send(ids_send, ids_recv, ids_out, ids_in)
        source = slot_column([atmos_ref[d : d + 1, :] for d in range(tiles)], cap)
        spread = jnp.broadcast_to(len_ref[...], (slots, tiles))
        owner = iota((slots, tiles), 1) == iota((slots, tiles), 0) // cap
        length = jnp.sum(jnp.where(owner, spread.astype(F32), 0.0), axis=1, keepdims=True)
        live = lax.rem(iota((slots, 1), 0), cap).astype(F32) < length
        place = one_hot((iota((slots, blocks), 1).astype(F32) == source) & live)
        picked = dot(place, surface_rows()).astype(BF16)
        fields = [picked[:, n * BLK : (n + 1) * BLK] for n in range(NF)]
        summed[...] = jnp.zeros_like(summed)

        @pl.loop(0, chunks)
        def _(q):
            weights = weights_ref[:, pl.ds(pl.multiple_of(q * MXU, MXU), MXU)].astype(F32)
            widen = one_hot(iota((BLK, MXU), 0) == q * per_chunk + iota((BLK, MXU), 1) // BLK)
            for n in range(NF):
                summed[n] += dot(fields[n], widen) * weights

        flux = jnp.zeros((slots, MXU), F32)
        for n in range(NF):
            fold = one_hot(iota((MXU, MXU), 1) == n * BLK + lax.rem(iota((MXU, MXU), 0), BLK))
            flux += dot(summed[n].astype(BF16), fold)
        data_send[...] = flux.astype(BF16).reshape(tiles, cap, MXU)
        send(data_send, data_recv, data_out, data_in)

        wait_all(data_recv, data_in)
        echoes = data_recv[...].reshape(slots, MXU)
        for n in range(NF):
            repeat = one_hot(iota((MXU, MXU), 0) == n * BLK + lax.rem(iota((MXU, MXU), 1), BLK))
            expanded[n] = dot(echoes, repeat)
        summed[:, :, 0:BLK] = jnp.zeros((NF, slots, BLK), F32)

        @pl.loop(0, chunks)
        def _(q):
            weights = weights_ref[:, pl.ds(pl.multiple_of(q * MXU, MXU), MXU)].astype(F32)
            gather = one_hot(iota((MXU, BLK), 1) == q * per_chunk + iota((MXU, BLK), 0) // BLK)
            for n in range(NF):
                summed[n, :, 0:BLK] += dot((expanded[n] * weights).astype(BF16), gather)

        back = jnp.concatenate([summed[n, :, 0:BLK] for n in range(NF)], axis=1)
        high = back.astype(BF16)
        low = (back - high.astype(F32)).astype(BF16)
        emit(dot(place, high, ((0,), (0,))) + dot(place, low, ((0,), (0,))))
        wait_all(ids_send, ids_out)
        wait_all(data_send, data_out)

    @pl.when(section == 1)
    def _():
        rows = surface_rows()
        wait_all(ids_recv, ids_in)
        wanted = slot_column([ids_recv[t, 0:1, :] for t in range(tiles)], cap)
        place = one_hot(owned_ref[...].astype(F32) == wanted)
        data_send[...] = dot(place, rows).astype(BF16).reshape(tiles, cap, MXU)
        send(data_send, data_recv, data_out, data_in)
        wait_all(data_recv, data_in)
        emit(dot(place, data_recv[...].reshape(slots, MXU), ((0,), (0,))))
        wait_all(data_send, data_out)


def exchange(surface, weights, pair_atmos, pair_ocean, list_len, owned):
    tiles, cap = pair_atmos.shape
    blocks = owned.shape[1]
    slots = tiles * cap
    return pl.pallas_call(
        functools.partial(exchange_kernel, tiles, cap),
        out_shape=jax.ShapeDtypeStruct((NF, blocks, BLK), F32),
        in_specs=[pl.BlockSpec(memory_space=pltpu.VMEM)] * 6,
        out_specs=pl.BlockSpec(memory_space=pltpu.VMEM),
        scratch_shapes=[
            pltpu.VMEM((tiles, 8, 128), jnp.int32),
            pltpu.VMEM((tiles, 8, 128), jnp.int32),
            pltpu.VMEM((tiles, cap, MXU), BF16),
            pltpu.VMEM((tiles, cap, MXU), BF16),
            pltpu.VMEM((NF, slots, MXU), F32),
            pltpu.VMEM((NF, slots, MXU), F32),
            pltpu.SemaphoreType.DMA((4,)),
        ],
        compiler_params=pltpu.CompilerParams(
            collective_id=0, has_side_effects=True, vmem_limit_bytes=48 * 1024 * 1024
        ),
        name="exchange",
    )(surface, weights, pair_atmos, pair_ocean, list_len, owned)


def sweep_kernel(levels, rows, group, lanes, units, state_ref, coef_ref, ops_ref, write_ref, forcing_ref, out_ref, big):
    steps = ops_ref.shape[0]
    full = big.shape[1]

    @pl.when(pl.program_id(0) == 0)
    def _():
        tiler = one_hot(
            (lax.rem(iota((rows, full), 1), rows) == iota((rows, full), 0)) & (iota((rows, full), 1) < group * rows)
        )
        lane = iota((rows, full), 1)
        for step in range(steps):
            tiled = dot(ops_ref[step], tiler)
            for part in range(group):
                inside = (lane >= part * rows) & (lane < (part + 1) * rows)
                big[step, part * rows : (part + 1) * rows, :] = jnp.where(inside, tiled, 0.0).astype(BF16)
            if full > group * rows:
                big[step, group * rows :, :] = jnp.zeros((full - group * rows, full), BF16)

    valid = iota((rows, lanes), 0) < levels

    def columns(unit, part):
        return pl.ds((unit * group + part) * lanes, lanes)

    def stacked(ref, unit):
        pieces = [jnp.where(valid, ref[0, :, columns(unit, part)].astype(F32), 0.0) for part in range(group)]
        if full > group * rows:
            pieces.append(jnp.zeros((full - group * rows, lanes), F32))
        return jnp.concatenate(pieces, axis=0).T

    current = [stacked(state_ref, unit).astype(BF16) for unit in range(units)]
    factors = [stacked(coef_ref, unit) for unit in range(units)]
    for step in range(steps):
        for unit in range(units):
            current[unit] = (dot(current[unit], big[step]) * factors[unit]).astype(BF16)

    write = write_ref[...]
    write_high = write.astype(BF16).astype(F32)
    write_parts = jnp.concatenate([write_high, write_high, write - write_high], axis=1).astype(BF16)
    for unit in range(units):
        swept = current[unit].astype(F32).T
        for part in range(group):
            forcing = forcing_ref[:, columns(unit, part)]
            high = forcing.astype(BF16).astype(F32)
            parts = jnp.concatenate([high, forcing - high, high], axis=0).astype(BF16)
            out_ref[0, :, columns(unit, part)] = (
                swept[part * rows : (part + 1) * rows] + dot(write_parts, parts)
            ).astype(BF16)


def sweep(state, coef, column_ops, surf_write, forcing):
    _, levels, cells = state.shape
    steps = column_ops.shape[1]
    rows = round_up(levels, 16)
    full = round_up(rows, MXU)
    group = full // rows
    lanes, units = next(
        (lanes, units)
        for lanes, units in ((512, 2), (512, 1), (256, 1), (128, 1))
        if cells % (group * lanes * units) == 0
    )
    block = group * lanes * units
    operators = jnp.pad(column_ops[0], ((0, 0), (0, rows - levels), (0, rows - levels)))
    write = jnp.pad(surf_write[0], ((0, rows - levels), (0, 0)))
    wide = pl.BlockSpec((1, rows, block), lambda i: (0, 0, i))
    return pl.pallas_call(
        functools.partial(sweep_kernel, levels, rows, group, lanes, units),
        out_shape=jax.ShapeDtypeStruct(state.shape, BF16),
        grid=(cells // block,),
        in_specs=[
            wide,
            wide,
            pl.BlockSpec(operators.shape, lambda i: (0, 0, 0)),
            pl.BlockSpec(write.shape, lambda i: (0, 0)),
            pl.BlockSpec((NF, block), lambda i: (0, i)),
        ],
        out_specs=wide,
        scratch_shapes=[pltpu.VMEM((steps, full, full), BF16)],
        compiler_params=pltpu.CompilerParams(
            dimension_semantics=("arbitrary",), vmem_limit_bytes=56 * 1024 * 1024
        ),
        name="sweep",
    )(state, coef, operators, write, forcing)


def body(
    adjoint_state,
    tangent_coef,
    column_ops,
    surf_read,
    surf_write,
    remap_weights,
    pair_atmos,
    pair_ocean,
    list_len,
    ocean_owned,
):
    tiles, cap = pair_atmos.shape[1:]
    blocks = ocean_owned.shape[1]
    surface = jnp.dot(surf_read[0], adjoint_state[0], preferred_element_type=F32).astype(BF16)
    forcing = exchange(
        surface.reshape(NF, blocks, BLK),
        remap_weights.reshape(tiles * cap, BLK * BLK),
        pair_atmos[0],
        pair_ocean[0],
        list_len,
        ocean_owned,
    )
    return sweep(adjoint_state, tangent_coef, column_ops, surf_write, forcing.reshape(NF, blocks * BLK))


def solution(mesh):
    in_specs = (
        P("sec", None, "tile"),
        P("sec", None, "tile"),
        P("sec", None, None, None),
        P("sec", None, None),
        P("sec", None, None),
        P("tile", None, None, None),
        P("tile", None, None),
        P("tile", None, None),
        P("tile", None),
        P("tile", None),
    )
    out_specs = P("sec", None, "tile")
    return jax.shard_map(body, mesh=mesh, in_specs=in_specs, out_specs=out_specs, check_vma=False)
```

```python
import functools

import jax
import jax.numpy as jnp
from jax import lax
from jax.experimental import pallas as pl
from jax.experimental.pallas import tpu as pltpu
from jax.sharding import PartitionSpec as P

NF = 4
BLK = 64
MXU = 256
MESH = pl.DeviceIdType.MESH
F32 = jnp.float32
BF16 = jnp.bfloat16


def round_up(value, unit):
    return -(-value // unit) * unit


def iota(shape, axis):
    return lax.broadcasted_iota(jnp.int32, shape, axis)


def dot(left, right, contract=((1,), (0,))):
    return lax.dot_general(left, right, (contract, ((), ())), preferred_element_type=F32)


def one_hot(condition):
    return jnp.where(condition, 1.0, 0.0).astype(BF16)


def slot_column(rows, cap):
    spread = jnp.concatenate([jnp.broadcast_to(row, (cap, row.shape[1])) for row in rows], axis=0)
    chosen = iota(spread.shape, 1) == lax.rem(iota(spread.shape, 0), cap)
    return jnp.sum(jnp.where(chosen, spread.astype(F32), 0.0), axis=1, keepdims=True)


def exchange_kernel(
    tiles, cap, surface_ref, weights_ref, atmos_ref, ocean_ref, len_ref, owned_ref, out_ref,
    ids_send, ids_recv, flux_send, flux_recv, reply_send, reply_recv, back_half, back_recv,
    expanded, summed, folded, sems,
):
    section = lax.axis_index("sec")
    me = lax.axis_index("tile")
    other = 1 - section
    slots = tiles * cap
    half = tiles // 2
    half_slots = half * cap
    pairs = surface_ref.shape[1]
    blocks = 2 * pairs
    wide = 2 * MXU
    chunks = weights_ref.shape[1] // wide
    per_chunk = wide // BLK
    ids_out, ids_in, flux_out, flux_in, reply_out, reply_in, back_out, back_in = [sems.at[i] for i in range(8)]

    def peer(i):
        return lax.rem(me + i, tiles)

    barrier = pltpu.get_barrier_semaphore()

    @pl.loop(0, tiles)
    def _(i):
        pl.semaphore_signal(barrier, inc=1, device_id=(other, peer(i)), device_id_type=MESH)

    @pl.when(section == 1)
    def _():
        @pl.loop(1, tiles)
        def _(i):
            pl.semaphore_signal(barrier, inc=1, device_id=(section, peer(i)), device_id_type=MESH)

        pl.semaphore_wait(barrier, 2 * tiles - 1)

    @pl.when(section == 0)
    def _():
        pl.semaphore_wait(barrier, tiles)

    def send(source, target, send_sem, recv_sem, first, to):
        @pl.loop(first, tiles)
        def _(i):
            pltpu.make_async_remote_copy(
                src_ref=source.at[peer(i)],
                dst_ref=target,
                send_sem=send_sem,
                recv_sem=recv_sem,
                device_id=(to, peer(i)),
                device_id_type=MESH,
            ).start()

    def wait_all(buffer, sem):
        pltpu.make_async_copy(buffer, buffer, sem).wait()

    def surface_rows():
        lower = [surface_ref[n, :, 0:BLK] for n in range(NF)]
        upper = [surface_ref[n, :, BLK : 2 * BLK] for n in range(NF)]
        return jnp.concatenate([jnp.concatenate(lower, axis=1), jnp.concatenate(upper, axis=1)], axis=0)

    def emit(forcing):
        for n in range(NF):
            lanes = slice(n * BLK, (n + 1) * BLK)
            out_ref[n] = jnp.concatenate([forcing[:pairs, lanes], forcing[pairs:, lanes]], axis=1)

    def weights_at(q, first, count):
        return weights_ref[first : first + count, pl.ds(pl.multiple_of(q * wide, wide), wide)].astype(F32)

    def back_terms(first):
        echoes = reply_recv[...].reshape(half_slots, MXU)
        for n in range(NF):
            repeat = one_hot(iota((MXU, MXU), 0) == n * BLK + lax.rem(iota((MXU, MXU), 1), BLK))
            expanded[n] = dot(echoes, repeat)
        folded[...] = jnp.zeros_like(folded)

        @pl.loop(0, chunks)
        def _(q):
            weights = weights_at(q, first, half_slots)
            gather = one_hot(iota((wide, BLK), 1) == q * per_chunk + iota((wide, BLK), 0) // BLK)
            for n in range(NF):
                copies = jnp.concatenate([expanded[n], expanded[n]], axis=1)
                folded[n] += dot((copies * weights).astype(BF16), gather)

        back_half[...] = jnp.concatenate([folded[n] for n in range(NF)], axis=1).astype(BF16)

    @pl.when(section == 0)
    def _():
        for d in range(tiles):
            ids_send[d, 0:1, 0:cap] = ocean_ref[d : d + 1, :]
        send(ids_send, ids_recv.at[me], ids_out, ids_in, 0, 1)
        source = slot_column([atmos_ref[d : d + 1, :] for d in range(tiles)], cap)
        spread = jnp.broadcast_to(len_ref[...], (slots, tiles))
        owner = iota((slots, tiles), 1) == iota((slots, tiles), 0) // cap
        length = jnp.sum(jnp.where(owner, spread.astype(F32), 0.0), axis=1, keepdims=True)
        live = lax.rem(iota((slots, 1), 0), cap).astype(F32) < length
        lane = iota((slots, blocks), 1)
        block = 2 * lax.rem(lane, pairs) + lane // pairs
        place = one_hot((block.astype(F32) == source) & live)
        picked = dot(place, surface_rows()).astype(BF16)
        fields = [picked[:, n * BLK : (n + 1) * BLK] for n in range(NF)]
        summed[...] = jnp.zeros_like(summed)

        @pl.loop(0, chunks)
        def _(q):
            weights = weights_at(q, 0, slots)
            widen = one_hot(iota((BLK, wide), 0) == q * per_chunk + iota((BLK, wide), 1) // BLK)
            for n in range(NF):
                terms = dot(fields[n], widen) * weights
                summed[n] += terms[:, :MXU] + terms[:, MXU:]

        flux = jnp.zeros((slots, MXU), F32)
        for n in range(NF):
            fold = one_hot(iota((MXU, MXU), 1) == n * BLK + lax.rem(iota((MXU, MXU), 0), BLK))
            flux += dot(summed[n].astype(BF16), fold)
        flux_send[...] = flux.astype(BF16).reshape(tiles, cap, MXU)
        send(flux_send, flux_recv.at[me], flux_out, flux_in, 0, 1)

        wait_all(reply_recv, reply_in)
        back_terms(0)
        wait_all(back_recv, back_in)
        back = jnp.concatenate([back_half[...], back_recv[...]], axis=0)
        emit(dot(place, back, ((0,), (0,))))
        wait_all(ids_send, ids_out)
        wait_all(flux_send, flux_out)

    @pl.when(section == 1)
    def _():
        rows = surface_rows()
        wait_all(ids_recv, ids_in)
        wanted = slot_column([ids_recv[t, 0:1, :] for t in range(tiles)], cap)
        place = one_hot(owned_ref[...].astype(F32) == wanted)
        reply_send[...] = dot(place, rows).astype(BF16).reshape(tiles, cap, MXU)
        upper = me >= half

        @pl.when(upper)
        def _():
            send(reply_send, reply_recv.at[me - half], reply_out, reply_in, 1, 1)
            reply_recv[me - half] = reply_send[me]
            wait_all(reply_recv.at[pl.ds(0, half - 1)], reply_in)

        @pl.when(jnp.logical_not(upper))
        def _():
            send(reply_send, reply_recv.at[me], reply_out, reply_in, 0, 0)
            wait_all(reply_recv, reply_in)

        back_terms(half_slots)
        back_copy = pltpu.make_async_remote_copy(
            src_ref=back_half,
            dst_ref=back_recv,
            send_sem=back_out,
            recv_sem=back_in,
            device_id=(other, me),
            device_id_type=MESH,
        )
        back_copy.start()
        wait_all(flux_recv, flux_in)
        emit(dot(place, flux_recv[...].reshape(slots, MXU), ((0,), (0,))))
        back_copy.wait_send()

        @pl.when(upper)
        def _():
            wait_all(reply_send.at[pl.ds(0, tiles - 1)], reply_out)

        @pl.when(jnp.logical_not(upper))
        def _():
            wait_all(reply_send, reply_out)


def exchange(surface, weights, pair_atmos, pair_ocean, list_len, owned):
    tiles, cap = pair_atmos.shape
    pairs = surface.shape[1]
    slots = tiles * cap
    half = tiles // 2
    return pl.pallas_call(
        functools.partial(exchange_kernel, tiles, cap),
        out_shape=jax.ShapeDtypeStruct((NF, pairs, 2 * BLK), F32),
        in_specs=[pl.BlockSpec(memory_space=pltpu.VMEM)] * 6,
        out_specs=pl.BlockSpec(memory_space=pltpu.VMEM),
        scratch_shapes=[
            pltpu.VMEM((tiles, 8, 128), jnp.int32),
            pltpu.VMEM((tiles, 8, 128), jnp.int32),
            pltpu.VMEM((tiles, cap, MXU), BF16),
            pltpu.VMEM((tiles, cap, MXU), BF16),
            pltpu.VMEM((tiles, cap, MXU), BF16),
            pltpu.VMEM((half, cap, MXU), BF16),
            pltpu.VMEM((half * cap, MXU), BF16),
            pltpu.VMEM((half * cap, MXU), BF16),
            pltpu.VMEM((NF, half * cap, MXU), F32),
            pltpu.VMEM((NF, slots, MXU), F32),
            pltpu.VMEM((NF, half * cap, BLK), F32),
            pltpu.SemaphoreType.DMA((8,)),
        ],
        compiler_params=pltpu.CompilerParams(
            collective_id=0, has_side_effects=True, vmem_limit_bytes=48 * 1024 * 1024
        ),
        name="exchange",
    )(surface, weights, pair_atmos, pair_ocean, list_len, owned)


def sweep_kernel(levels, rows, group, lanes, units, state_ref, coef_ref, ops_ref, write_ref, forcing_ref, out_ref, big):
    steps = ops_ref.shape[0]
    full = big.shape[1]

    @pl.when(pl.program_id(0) == 0)
    def _():
        tiler = one_hot(
            (lax.rem(iota((levels, full), 1), rows) == iota((levels, full), 0))
            & (iota((levels, full), 1) < group * rows)
        )
        valid = iota((rows, levels), 0) < levels
        lane = iota((rows, full), 1)
        for step in range(steps):
            operator = jnp.where(valid, ops_ref[step].astype(F32), 0.0).astype(BF16)
            tiled = dot(operator, tiler)
            for part in range(group):
                inside = (lane >= part * rows) & (lane < (part + 1) * rows)
                big[step, part * rows : (part + 1) * rows, :] = jnp.where(inside, tiled, 0.0).astype(BF16)
            if full > group * rows:
                big[step, group * rows :, :] = jnp.zeros((full - group * rows, full), BF16)

    valid = iota((rows, lanes), 0) < levels

    def columns(unit, part):
        return pl.ds((unit * group + part) * lanes, lanes)

    def stacked(ref, unit):
        pieces = [
            jnp.where(valid, ref[0, :, columns(unit, part)].astype(F32), 0.0).astype(BF16) for part in range(group)
        ]
        if full > group * rows:
            pieces.append(jnp.zeros((full - group * rows, lanes), BF16))
        return jnp.concatenate(pieces, axis=0).T

    current = [stacked(state_ref, unit) for unit in range(units)]
    factors = [stacked(coef_ref, unit).astype(F32) for unit in range(units)]
    for step in range(steps):
        for unit in range(units):
            current[unit] = (dot(current[unit], big[step]) * factors[unit]).astype(BF16)

    write = write_ref[:, 0:rows]
    write_high = write.astype(BF16).astype(F32)
    write_parts = jnp.concatenate([write_high, write_high, write - write_high], axis=0).astype(BF16)
    for unit in range(units):
        swept = current[unit].T.astype(F32)
        for part in range(group):
            forcing = forcing_ref[:, columns(unit, part)]
            high = forcing.astype(BF16).astype(F32)
            parts = jnp.concatenate([high, forcing - high, high], axis=0).astype(BF16)
            out_ref[0, :, columns(unit, part)] = (
                swept[part * rows : (part + 1) * rows] + dot(write_parts, parts, ((0,), (0,)))
            ).astype(BF16)


def sweep(state, coef, column_ops, surf_write, forcing):
    _, levels, cells = state.shape
    steps = column_ops.shape[1]
    rows = round_up(levels, 16)
    full = round_up(rows, MXU)
    group = full // rows
    lanes, units = next(
        (lanes, units)
        for lanes, units in ((1024, 2), (512, 2), (512, 1), (256, 1), (128, 1))
        if cells % (group * lanes * units) == 0
    )
    block = group * lanes * units
    operators = column_ops[0]
    write = surf_write[0].T
    wide = pl.BlockSpec((1, rows, block), lambda i: (0, 0, i))
    return pl.pallas_call(
        functools.partial(sweep_kernel, levels, rows, group, lanes, units),
        out_shape=jax.ShapeDtypeStruct(state.shape, BF16),
        grid=(cells // block,),
        in_specs=[
            wide,
            wide,
            pl.BlockSpec((steps, rows, levels), lambda i: (0, 0, 0)),
            pl.BlockSpec((NF, round_up(rows, 128)), lambda i: (0, 0)),
            pl.BlockSpec((NF, block), lambda i: (0, i)),
        ],
        out_specs=wide,
        scratch_shapes=[pltpu.VMEM((steps, full, full), BF16)],
        compiler_params=pltpu.CompilerParams(
            dimension_semantics=("arbitrary",), vmem_limit_bytes=56 * 1024 * 1024
        ),
        name="sweep",
    )(state, coef, operators, write, forcing)


def body(
    adjoint_state,
    tangent_coef,
    column_ops,
    surf_read,
    surf_write,
    remap_weights,
    pair_atmos,
    pair_ocean,
    list_len,
    ocean_owned,
):
    tiles, cap = pair_atmos.shape[1:]
    pairs = ocean_owned.shape[1] // 2
    surface = jnp.dot(surf_read[0], adjoint_state[0], preferred_element_type=F32).astype(BF16)
    owned = jnp.swapaxes(ocean_owned.reshape(pairs, 2), 0, 1).reshape(1, 2 * pairs)
    forcing = exchange(
        surface.reshape(NF, pairs, 2 * BLK),
        remap_weights.reshape(tiles * cap, BLK * BLK),
        pair_atmos[0],
        pair_ocean[0],
        list_len,
        owned,
    )
    return sweep(adjoint_state, tangent_coef, column_ops, surf_write, forcing.reshape(NF, 2 * pairs * BLK))


def solution(mesh):
    in_specs = (
        P("sec", None, "tile"),
        P("sec", None, "tile"),
        P("sec", None, None, None),
        P("sec", None, None),
        P("sec", None, None),
        P("tile", None, None, None),
        P("tile", None, None),
        P("tile", None, None),
        P("tile", None),
        P("tile", None),
    )
    out_specs = P("sec", None, "tile")
    return jax.shard_map(body, mesh=mesh, in_specs=in_specs, out_specs=out_specs, check_vma=False)
```

```python
import functools

import jax
import jax.numpy as jnp
from jax import lax
from jax.experimental import pallas as pl
from jax.experimental.pallas import tpu as pltpu
from jax.sharding import PartitionSpec as P

NF = 4
BLK = 64
MXU = 256
MESH = pl.DeviceIdType.MESH
F32 = jnp.float32
BF16 = jnp.bfloat16


def round_up(value, unit):
    return -(-value // unit) * unit


def iota(shape, axis):
    return lax.broadcasted_iota(jnp.int32, shape, axis)


def dot(left, right, contract=((1,), (0,))):
    return lax.dot_general(left, right, (contract, ((), ())), preferred_element_type=F32)


def one_hot(condition):
    return jnp.where(condition, 1.0, 0.0).astype(BF16)


def slot_column(rows, cap):
    spread = jnp.concatenate([jnp.broadcast_to(row, (cap, row.shape[1])) for row in rows], axis=0)
    chosen = iota(spread.shape, 1) == lax.rem(iota(spread.shape, 0), cap)
    return jnp.sum(jnp.where(chosen, spread.astype(F32), 0.0), axis=1, keepdims=True)


def build_operators(levels, rows, group, ops_ref, big):
    full = big.shape[1]
    lane = iota((rows, full), 1)
    target = iota((levels, full), 1)
    tiler = one_hot((lax.rem(target, rows) == iota((levels, full), 0)) & (target < group * rows))
    blank = jnp.zeros((rows - levels, levels), F32)
    for step in range(ops_ref.shape[0]):
        operator = jnp.concatenate([ops_ref[step].astype(F32), blank], axis=0).astype(BF16)
        tiled = dot(operator, tiler)
        for part in range(group):
            inside = (lane >= part * rows) & (lane < (part + 1) * rows)
            big[step, part * rows : (part + 1) * rows, :] = jnp.where(inside, tiled, 0.0).astype(BF16)
        if full > group * rows:
            big[step, group * rows :, :] = jnp.zeros((full - group * rows, full), BF16)


def stack_columns(pieces, full):
    stacked = sum(piece.shape[0] for piece in pieces)
    if full > stacked:
        pieces = pieces + [jnp.zeros((full - stacked, pieces[0].shape[1]), BF16)]
    return jnp.concatenate(pieces, axis=0).T


def all_steps(current, factors, big):
    for step in range(big.shape[0]):
        for unit in range(len(current)):
            current[unit] = (dot(current[unit], big[step]) * factors[unit]).astype(BF16)
    return current


def exchange_kernel(
    tiles, cap, levels, rows, group, lanes, units,
    surface_ref, weights_ref, atmos_ref, ocean_ref, len_ref, owned_ref, state_ref, coef_ref, ops_ref,
    out_ref, swept_ref,
    ids_send, ids_recv, flux_send, flux_recv, reply_send, reply_recv, back_half, back_recv, place_buf,
    expanded, summed, folded, state_buf, coef_buf, big, sems, load_sems,
):
    section = lax.axis_index("sec")
    me = lax.axis_index("tile")
    other = 1 - section
    slots = tiles * cap
    half = tiles // 2
    half_slots = half * cap
    pairs = surface_ref.shape[1]
    blocks = 2 * pairs
    wide = 2 * MXU
    chunks = weights_ref.shape[1] // wide
    per_chunk = wide // BLK
    ids_out, ids_in, flux_out, flux_in, reply_out, reply_in, back_out, back_in = [sems.at[i] for i in range(8)]

    def peer(i):
        return lax.rem(me + i, tiles)

    early = swept_ref.shape[0]
    block_cells = group * lanes * units
    full = big.shape[1]

    def load(source, target, kind, j):
        start = pl.multiple_of(j * block_cells, block_cells)
        return pltpu.make_async_copy(
            source.at[0, :, pl.ds(start, block_cells)], target.at[j], load_sems.at[kind, j]
        )

    for j in range(early):
        load(state_ref, state_buf, 0, j).start()
        load(coef_ref, coef_buf, 1, j).start()

    def sweep_blocks(first, last):
        @pl.loop(first, last)
        def _(j):
            load(state_ref, state_buf, 0, j).wait()
            load(coef_ref, coef_buf, 1, j).wait()

            def columns(unit, part):
                return pl.ds((unit * group + part) * lanes, lanes)

            def stacked(buffer, unit):
                pieces = []
                for part in range(group):
                    piece = buffer[j, :, columns(unit, part)].astype(F32)
                    blank = jnp.zeros((rows - levels, lanes), F32)
                    pieces.append(jnp.concatenate([piece, blank], axis=0).astype(BF16))
                return stack_columns(pieces, full)

            current = [stacked(state_buf, unit) for unit in range(units)]
            factors = [stacked(coef_buf, unit).astype(F32) for unit in range(units)]
            current = all_steps(current, factors, big)
            for unit in range(units):
                swept = current[unit].T
                for part in range(group):
                    swept_ref[j, :, columns(unit, part)] = swept[part * rows : (part + 1) * rows]

    barrier = pltpu.get_barrier_semaphore()

    @pl.loop(0, tiles)
    def _(i):
        pl.semaphore_signal(barrier, inc=1, device_id=(other, peer(i)), device_id_type=MESH)

    @pl.when(section == 1)
    def _():
        @pl.loop(1, tiles)
        def _(i):
            pl.semaphore_signal(barrier, inc=1, device_id=(section, peer(i)), device_id_type=MESH)

    def send(source, target, send_sem, recv_sem, first, to):
        @pl.loop(first, tiles)
        def _(i):
            pltpu.make_async_remote_copy(
                src_ref=source.at[peer(i)],
                dst_ref=target,
                send_sem=send_sem,
                recv_sem=recv_sem,
                device_id=(to, peer(i)),
                device_id_type=MESH,
            ).start()

    def wait_all(buffer, sem):
        pltpu.make_async_copy(buffer, buffer, sem).wait()

    def surface_rows():
        lower = [surface_ref[n, :, 0:BLK] for n in range(NF)]
        upper = [surface_ref[n, :, BLK : 2 * BLK] for n in range(NF)]
        return jnp.concatenate([jnp.concatenate(lower, axis=1), jnp.concatenate(upper, axis=1)], axis=0)

    def emit(forcing):
        for n in range(NF):
            lanes = slice(n * BLK, (n + 1) * BLK)
            out_ref[:, n, :] = jnp.concatenate([forcing[:pairs, lanes], forcing[pairs:, lanes]], axis=1)

    def weights_at(q, first, count):
        return weights_ref[first : first + count, pl.ds(pl.multiple_of(q * wide, wide), wide)].astype(F32)

    def back_terms(first):
        echoes = reply_recv[...].reshape(half_slots, MXU)
        for n in range(NF):
            repeat = one_hot(iota((MXU, MXU), 0) == n * BLK + lax.rem(iota((MXU, MXU), 1), BLK))
            expanded[n] = dot(echoes, repeat)
        folded[...] = jnp.zeros_like(folded)

        @pl.loop(0, chunks)
        def _(q):
            weights = weights_at(q, first, half_slots)
            gather = one_hot(iota((wide, BLK), 1) == q * per_chunk + iota((wide, BLK), 0) // BLK)
            for n in range(NF):
                copies = jnp.concatenate([expanded[n], expanded[n]], axis=1)
                folded[n] += dot((copies * weights).astype(BF16), gather)

        back_half[...] = jnp.concatenate([folded[n] for n in range(NF)], axis=1).astype(BF16)

    build_operators(levels, rows, group, ops_ref, big)

    @pl.when(section == 0)
    def _():
        for d in range(tiles):
            ids_send[d, 0:1, 0:cap] = ocean_ref[d : d + 1, :]
        source = slot_column([atmos_ref[d : d + 1, :] for d in range(tiles)], cap)
        spread = jnp.broadcast_to(len_ref[...], (slots, tiles))
        owner = iota((slots, tiles), 1) == iota((slots, tiles), 0) // cap
        length = jnp.sum(jnp.where(owner, spread.astype(F32), 0.0), axis=1, keepdims=True)
        live = lax.rem(iota((slots, 1), 0), cap).astype(F32) < length
        lane = iota((slots, blocks), 1)
        block = 2 * lax.rem(lane, pairs) + lane // pairs
        place = one_hot((block.astype(F32) == source) & live)
        place_buf[...] = place
        picked = dot(place, surface_rows()).astype(BF16)
        fields = [picked[:, n * BLK : (n + 1) * BLK] for n in range(NF)]
        summed[...] = jnp.zeros_like(summed)

        @pl.loop(0, chunks)
        def _(q):
            weights = weights_at(q, 0, slots)
            widen = one_hot(iota((BLK, wide), 0) == q * per_chunk + iota((BLK, wide), 1) // BLK)
            for n in range(NF):
                terms = dot(fields[n], widen) * weights
                summed[n] += terms[:, :MXU] + terms[:, MXU:]

        flux = jnp.zeros((slots, MXU), F32)
        for n in range(NF):
            fold = one_hot(iota((MXU, MXU), 1) == n * BLK + lax.rem(iota((MXU, MXU), 0), BLK))
            flux += dot(summed[n].astype(BF16), fold)
        flux_send[...] = flux.astype(BF16).reshape(tiles, cap, MXU)

    third = early // 3
    middle = third * (1 + section)
    sweep_blocks(0, middle)

    @pl.when(section == 0)
    def _():
        pl.semaphore_wait(barrier, tiles)
        send(ids_send, ids_recv.at[me], ids_out, ids_in, 0, 1)
        send(flux_send, flux_recv.at[me], flux_out, flux_in, 0, 1)

    @pl.when(section == 1)
    def _():
        pl.semaphore_wait(barrier, 2 * tiles - 1)
        surface = surface_rows()
        wait_all(ids_recv, ids_in)
        wanted = slot_column([ids_recv[t, 0:1, :] for t in range(tiles)], cap)
        place = one_hot(owned_ref[...].astype(F32) == wanted)
        place_buf[...] = place
        reply_send[...] = dot(place, surface).astype(BF16).reshape(tiles, cap, MXU)

        @pl.when(me >= half)
        def _():
            send(reply_send, reply_recv.at[me - half], reply_out, reply_in, 1, 1)
            reply_recv[me - half] = reply_send[me]

        @pl.when(me < half)
        def _():
            send(reply_send, reply_recv.at[me], reply_out, reply_in, 0, 0)

    sweep_blocks(middle, early)

    @pl.when(section == 0)
    def _():
        wait_all(reply_recv, reply_in)
        back_terms(0)
        wait_all(back_recv, back_in)
        back = jnp.concatenate([back_half[...], back_recv[...]], axis=0)
        emit(dot(place_buf[...], back, ((0,), (0,))))
        wait_all(ids_send, ids_out)
        wait_all(flux_send, flux_out)

    @pl.when(section == 1)
    def _():
        upper = me >= half

        @pl.when(upper)
        def _():
            wait_all(reply_recv.at[pl.ds(0, half - 1)], reply_in)

        @pl.when(jnp.logical_not(upper))
        def _():
            wait_all(reply_recv, reply_in)

        back_terms(half_slots)
        back_copy = pltpu.make_async_remote_copy(
            src_ref=back_half,
            dst_ref=back_recv,
            send_sem=back_out,
            recv_sem=back_in,
            device_id=(other, me),
            device_id_type=MESH,
        )
        back_copy.start()
        wait_all(flux_recv, flux_in)
        emit(dot(place_buf[...], flux_recv[...].reshape(slots, MXU), ((0,), (0,))))
        back_copy.wait_send()

        @pl.when(upper)
        def _():
            wait_all(reply_send.at[pl.ds(0, tiles - 1)], reply_out)

        @pl.when(jnp.logical_not(upper))
        def _():
            wait_all(reply_send, reply_out)


def layout(levels, cells):
    rows = round_up(levels, 16)
    full = round_up(rows, MXU)
    group = full // rows
    lanes = next(lanes for lanes in (512, 256, 128) if cells % (4 * group * lanes) == 0)
    return rows, full, group, lanes, 2


def exchange(surface, weights, pair_atmos, pair_ocean, list_len, owned, state, coef, operators):
    tiles, cap = pair_atmos.shape
    pairs = surface.shape[1]
    slots = tiles * cap
    half = tiles // 2
    _, levels, cells = state.shape
    steps = operators.shape[0]
    rows, full, group, lanes, units = layout(levels, cells)
    block = group * lanes * units
    early = cells // block // 2
    in_vmem = pl.BlockSpec(memory_space=pltpu.VMEM)
    in_place = pl.BlockSpec(memory_space=pl.ANY)
    return pl.pallas_call(
        functools.partial(exchange_kernel, tiles, cap, levels, rows, group, lanes, units),
        out_shape=(
            jax.ShapeDtypeStruct((pairs, NF, 2 * BLK), F32),
            jax.ShapeDtypeStruct((early, rows, block), BF16),
        ),
        in_specs=[in_vmem] * 6 + [in_place] * 2 + [in_vmem],
        out_specs=(in_vmem, in_vmem),
        scratch_shapes=[
            pltpu.VMEM((tiles, 8, 128), jnp.int32),
            pltpu.VMEM((tiles, 8, 128), jnp.int32),
            pltpu.VMEM((tiles, cap, MXU), BF16),
            pltpu.VMEM((tiles, cap, MXU), BF16),
            pltpu.VMEM((tiles, cap, MXU), BF16),
            pltpu.VMEM((half, cap, MXU), BF16),
            pltpu.VMEM((half * cap, MXU), BF16),
            pltpu.VMEM((half * cap, MXU), BF16),
            pltpu.VMEM((slots, 2 * pairs), BF16),
            pltpu.VMEM((NF, half * cap, MXU), F32),
            pltpu.VMEM((NF, slots, MXU), F32),
            pltpu.VMEM((NF, half * cap, BLK), F32),
            pltpu.VMEM((early, levels, block), BF16),
            pltpu.VMEM((early, levels, block), BF16),
            pltpu.VMEM((steps, full, full), BF16),
            pltpu.SemaphoreType.DMA((8,)),
            pltpu.SemaphoreType.DMA((2, early)),
        ],
        compiler_params=pltpu.CompilerParams(
            collective_id=0, has_side_effects=True, vmem_limit_bytes=56 * 1024 * 1024
        ),
        name="exchange",
    )(surface, weights, pair_atmos, pair_ocean, list_len, owned, state, coef, operators)


def sweep_kernel(
    levels, rows, group, lanes, units, early,
    state_ref, coef_ref, ops_ref, write_ref, forcing_ref, swept_ref, out_ref, big,
):
    index = pl.program_id(0)
    full = big.shape[1]

    @pl.when(index == 0)
    def _():
        build_operators(levels, rows, group, ops_ref, big)

    def columns(unit, part):
        return pl.ds((unit * group + part) * lanes, lanes)

    write = write_ref[:, 0:rows]
    write_high = write.astype(BF16).astype(F32)
    write_parts = jnp.concatenate([write_high, write_high, write - write_high], axis=0).astype(BF16)

    def finish(swept, unit, part):
        first = (unit * group + part) * lanes // (2 * BLK)
        forcing = jnp.concatenate([forcing_ref[first + r] for r in range(lanes // (2 * BLK))], axis=1)
        high = forcing.astype(BF16).astype(F32)
        parts = jnp.concatenate([high, forcing - high, high], axis=0).astype(BF16)
        added = dot(write_parts, parts, ((0,), (0,)))
        out_ref[0, :, columns(unit, part)] = (swept.astype(F32) + added).astype(BF16)

    @pl.when(index < early)
    def _():
        half = units // 2
        for unit in range(units):
            for part in range(group):
                finish(swept_ref[unit // half, :, columns(unit % half, part)], unit, part)

    @pl.when(index >= early)
    def _():
        valid = iota((rows, lanes), 0) < levels

        def stacked(ref, unit):
            pieces = [
                jnp.where(valid, ref[0, :, columns(unit, part)].astype(F32), 0.0).astype(BF16)
                for part in range(group)
            ]
            return stack_columns(pieces, full)

        current = [stacked(state_ref, unit) for unit in range(units)]
        factors = [stacked(coef_ref, unit).astype(F32) for unit in range(units)]
        current = all_steps(current, factors, big)
        for unit in range(units):
            swept = current[unit].T
            for part in range(group):
                finish(swept[part * rows : (part + 1) * rows], unit, part)


def sweep(state, coef, operators, surf_write, forcing, swept):
    _, levels, cells = state.shape
    steps = operators.shape[0]
    rows, full, group, lanes, units = layout(levels, cells)
    units = 2 * units
    block = group * lanes * units
    early = swept.shape[0] // 2
    wide = pl.BlockSpec((1, rows, block), lambda i: (0, 0, jnp.maximum(i, early)))
    return pl.pallas_call(
        functools.partial(sweep_kernel, levels, rows, group, lanes, units, early),
        out_shape=jax.ShapeDtypeStruct(state.shape, BF16),
        grid=(cells // block,),
        in_specs=[
            wide,
            wide,
            pl.BlockSpec(operators.shape, lambda i: (0, 0, 0)),
            pl.BlockSpec((NF, round_up(rows, 128)), lambda i: (0, 0)),
            pl.BlockSpec((block // (2 * BLK), NF, 2 * BLK), lambda i: (i, 0, 0)),
            pl.BlockSpec((2, rows, block // 2), lambda i: (jnp.minimum(i, early - 1), 0, 0)),
        ],
        out_specs=pl.BlockSpec((1, rows, block), lambda i: (0, 0, i)),
        scratch_shapes=[pltpu.VMEM((steps, full, full), BF16)],
        compiler_params=pltpu.CompilerParams(
            dimension_semantics=("arbitrary",), vmem_limit_bytes=56 * 1024 * 1024
        ),
        name="sweep",
    )(state, coef, operators, surf_write[0].T, forcing, swept)


def body(
    adjoint_state,
    tangent_coef,
    column_ops,
    surf_read,
    surf_write,
    remap_weights,
    pair_atmos,
    pair_ocean,
    list_len,
    ocean_owned,
):
    tiles, cap = pair_atmos.shape[1:]
    pairs = ocean_owned.shape[1] // 2
    surface = jnp.dot(surf_read[0], adjoint_state[0], preferred_element_type=F32).astype(BF16)
    owned = jnp.swapaxes(ocean_owned.reshape(pairs, 2), 0, 1).reshape(1, 2 * pairs)
    forcing, swept = exchange(
        surface.reshape(NF, pairs, 2 * BLK),
        remap_weights.reshape(tiles * cap, BLK * BLK),
        pair_atmos[0],
        pair_ocean[0],
        list_len,
        owned,
        adjoint_state,
        tangent_coef,
        column_ops[0],
    )
    return sweep(adjoint_state, tangent_coef, column_ops[0], surf_write, forcing, swept)


def solution(mesh):
    in_specs = (
        P("sec", None, "tile"),
        P("sec", None, "tile"),
        P("sec", None, None, None),
        P("sec", None, None),
        P("sec", None, None),
        P("tile", None, None, None),
        P("tile", None, None),
        P("tile", None, None),
        P("tile", None),
        P("tile", None),
    )
    out_specs = P("sec", None, "tile")
    return jax.shard_map(body, mesh=mesh, in_specs=in_specs, out_specs=out_specs, check_vma=False)
```

```python
import functools

import jax
import jax.numpy as jnp
from jax import lax
from jax.experimental import pallas as pl
from jax.experimental.pallas import tpu as pltpu
from jax.sharding import PartitionSpec as P

NF = 4
BLK = 64
MXU = 256
MESH = pl.DeviceIdType.MESH
F32 = jnp.float32
BF16 = jnp.bfloat16


def round_up(value, unit):
    return -(-value // unit) * unit


def iota(shape, axis):
    return lax.broadcasted_iota(jnp.int32, shape, axis)


def dot(left, right, contract=((1,), (0,))):
    return lax.dot_general(left, right, (contract, ((), ())), preferred_element_type=F32)


def one_hot(condition):
    return jnp.where(condition, 1.0, 0.0).astype(BF16)


def slot_column(rows, cap):
    spread = jnp.concatenate([jnp.broadcast_to(row, (cap, row.shape[1])) for row in rows], axis=0)
    chosen = iota(spread.shape, 1) == lax.rem(iota(spread.shape, 0), cap)
    return jnp.sum(jnp.where(chosen, spread.astype(F32), 0.0), axis=1, keepdims=True)


def build_operators(levels, rows, group, ops_ref, big):
    full = big.shape[1]
    lane = iota((rows, full), 1)
    target = iota((levels, full), 1)
    tiler = one_hot((lax.rem(target, rows) == iota((levels, full), 0)) & (target < group * rows))
    blank = jnp.zeros((rows - levels, levels), F32)
    for step in range(ops_ref.shape[0]):
        operator = jnp.concatenate([ops_ref[step].astype(F32), blank], axis=0).astype(BF16)
        tiled = dot(operator, tiler)
        for part in range(group):
            inside = (lane >= part * rows) & (lane < (part + 1) * rows)
            big[step, part * rows : (part + 1) * rows, :] = jnp.where(inside, tiled, 0.0).astype(BF16)
        if full > group * rows:
            big[step, group * rows :, :] = jnp.zeros((full - group * rows, full), BF16)


def stack_columns(pieces, full):
    stacked = sum(piece.shape[0] for piece in pieces)
    if full > stacked:
        pieces = pieces + [jnp.zeros((full - stacked, pieces[0].shape[1]), BF16)]
    return jnp.concatenate(pieces, axis=0).T


def all_steps(current, factors, big):
    for step in range(big.shape[0]):
        for unit in range(len(current)):
            current[unit] = (dot(current[unit], big[step]) * factors[unit]).astype(BF16)
    return current


def exchange_kernel(
    tiles, cap, levels, rows, group, lanes, units,
    surface_ref, weights_ref, atmos_ref, ocean_ref, len_ref, owned_ref, state_ref, coef_ref, ops_ref,
    out_ref, swept_ref,
    ids_send, ids_recv, flux_send, flux_recv, reply_send, reply_recv, back_half, back_recv, place_buf,
    expanded, summed, folded, state_buf, coef_buf, big, sems, load_sems,
):
    section = lax.axis_index("sec")
    me = lax.axis_index("tile")
    other = 1 - section
    slots = tiles * cap
    half = tiles // 2
    half_slots = half * cap
    pairs = surface_ref.shape[1]
    blocks = 2 * pairs
    wide = 2 * MXU
    chunks = weights_ref.shape[1] // wide
    per_chunk = wide // BLK
    ids_out, ids_in, flux_out, flux_in, reply_out, reply_in, back_out, back_in = [sems.at[i] for i in range(8)]

    def peer(i):
        return lax.rem(me + i, tiles)

    early = swept_ref.shape[0]
    block_cells = group * lanes * units
    full = big.shape[1]

    def load(source, target, kind, j):
        start = pl.multiple_of(j * block_cells, block_cells)
        return pltpu.make_async_copy(
            source.at[0, :, pl.ds(start, block_cells)], target.at[j], load_sems.at[kind, j]
        )

    for j in range(early):
        load(state_ref, state_buf, 0, j).start()
        load(coef_ref, coef_buf, 1, j).start()

    def sweep_blocks(first, last):
        @pl.loop(first, last)
        def _(j):
            load(state_ref, state_buf, 0, j).wait()
            load(coef_ref, coef_buf, 1, j).wait()

            def columns(unit, part):
                return pl.ds((unit * group + part) * lanes, lanes)

            def stacked(buffer, unit):
                pieces = []
                for part in range(group):
                    piece = buffer[j, :, columns(unit, part)].astype(F32)
                    blank = jnp.zeros((rows - levels, lanes), F32)
                    pieces.append(jnp.concatenate([piece, blank], axis=0).astype(BF16))
                return stack_columns(pieces, full)

            current = [stacked(state_buf, unit) for unit in range(units)]
            factors = [stacked(coef_buf, unit).astype(F32) for unit in range(units)]
            current = all_steps(current, factors, big)
            for unit in range(units):
                swept_ref[j, unit * lanes : (unit + 1) * lanes, :] = current[unit]

    barrier = pltpu.get_barrier_semaphore()

    @pl.loop(0, tiles)
    def _(i):
        pl.semaphore_signal(barrier, inc=1, device_id=(other, peer(i)), device_id_type=MESH)

    @pl.when(section == 1)
    def _():
        @pl.loop(1, tiles)
        def _(i):
            pl.semaphore_signal(barrier, inc=1, device_id=(section, peer(i)), device_id_type=MESH)

    def send(source, target, send_sem, recv_sem, first, to):
        @pl.loop(first, tiles)
        def _(i):
            pltpu.make_async_remote_copy(
                src_ref=source.at[peer(i)],
                dst_ref=target,
                send_sem=send_sem,
                recv_sem=recv_sem,
                device_id=(to, peer(i)),
                device_id_type=MESH,
            ).start()

    def wait_all(buffer, sem):
        pltpu.make_async_copy(buffer, buffer, sem).wait()

    def surface_rows():
        lower = [surface_ref[n, :, 0:BLK] for n in range(NF)]
        upper = [surface_ref[n, :, BLK : 2 * BLK] for n in range(NF)]
        return jnp.concatenate([jnp.concatenate(lower, axis=1), jnp.concatenate(upper, axis=1)], axis=0)

    def emit(forcing):
        for n in range(NF):
            lanes = slice(n * BLK, (n + 1) * BLK)
            out_ref[:, n, :] = jnp.concatenate([forcing[:pairs, lanes], forcing[pairs:, lanes]], axis=1)

    def weights_at(q, first, count):
        return weights_ref[first : first + count, pl.ds(pl.multiple_of(q * wide, wide), wide)].astype(F32)

    def back_terms(first):
        echoes = reply_recv[...].reshape(half_slots, MXU)
        for n in range(NF):
            repeat = one_hot(iota((MXU, MXU), 0) == n * BLK + lax.rem(iota((MXU, MXU), 1), BLK))
            expanded[n] = dot(echoes, repeat)
        folded[...] = jnp.zeros_like(folded)

        @pl.loop(0, chunks)
        def _(q):
            weights = weights_at(q, first, half_slots)
            gather = one_hot(iota((wide, BLK), 1) == q * per_chunk + iota((wide, BLK), 0) // BLK)
            products = []
            for n in range(NF):
                copies = jnp.concatenate([expanded[n], expanded[n]], axis=1)
                products.append((copies * weights).astype(BF16))
            folded[...] += dot(jnp.concatenate(products, axis=0), gather)

        fields = [folded[n * half_slots : (n + 1) * half_slots] for n in range(NF)]
        back_half[...] = jnp.concatenate(fields, axis=1).astype(BF16)

    build_operators(levels, rows, group, ops_ref, big)

    @pl.when(section == 0)
    def _():
        for d in range(tiles):
            ids_send[d, 0:1, 0:cap] = ocean_ref[d : d + 1, :]
        source = slot_column([atmos_ref[d : d + 1, :] for d in range(tiles)], cap)
        spread = jnp.broadcast_to(len_ref[...], (slots, tiles))
        owner = iota((slots, tiles), 1) == iota((slots, tiles), 0) // cap
        length = jnp.sum(jnp.where(owner, spread.astype(F32), 0.0), axis=1, keepdims=True)
        live = lax.rem(iota((slots, 1), 0), cap).astype(F32) < length
        lane = iota((slots, blocks), 1)
        block = 2 * lax.rem(lane, pairs) + lane // pairs
        place = one_hot((block.astype(F32) == source) & live)
        place_buf[...] = place
        picked = dot(place, surface_rows()).astype(BF16)
        fields = jnp.concatenate([picked[:, n * BLK : (n + 1) * BLK] for n in range(NF)], axis=0)
        summed[...] = jnp.zeros_like(summed)

        @pl.loop(0, chunks)
        def _(q):
            weights = weights_at(q, 0, slots)
            widen = one_hot(iota((BLK, wide), 0) == q * per_chunk + iota((BLK, wide), 1) // BLK)
            widened = dot(fields, widen)
            for n in range(NF):
                terms = widened[n * slots : (n + 1) * slots] * weights
                summed[n] += terms[:, :MXU] + terms[:, MXU:]

        flux = jnp.zeros((slots, MXU), F32)
        for n in range(NF):
            fold = one_hot(iota((MXU, MXU), 1) == n * BLK + lax.rem(iota((MXU, MXU), 0), BLK))
            flux += dot(summed[n].astype(BF16), fold)
        flux_send[...] = flux.astype(BF16).reshape(tiles, cap, MXU)

    middle = section * (2 * early // 3)
    sweep_blocks(0, middle)

    @pl.when(section == 0)
    def _():
        pl.semaphore_wait(barrier, tiles)
        send(ids_send, ids_recv.at[me], ids_out, ids_in, 0, 1)
        send(flux_send, flux_recv.at[me], flux_out, flux_in, 0, 1)

    @pl.when(section == 1)
    def _():
        pl.semaphore_wait(barrier, 2 * tiles - 1)
        surface = surface_rows()
        wait_all(ids_recv, ids_in)
        wanted = slot_column([ids_recv[t, 0:1, :] for t in range(tiles)], cap)
        place = one_hot(owned_ref[...].astype(F32) == wanted)
        place_buf[...] = place
        reply_send[...] = dot(place, surface).astype(BF16).reshape(tiles, cap, MXU)

        @pl.when(me >= half)
        def _():
            send(reply_send, reply_recv.at[me - half], reply_out, reply_in, 1, 1)
            reply_recv[me - half] = reply_send[me]

        @pl.when(me < half)
        def _():
            send(reply_send, reply_recv.at[me], reply_out, reply_in, 0, 0)

    sweep_blocks(middle, early)

    @pl.when(section == 0)
    def _():
        wait_all(reply_recv, reply_in)
        back_terms(0)
        wait_all(back_recv, back_in)
        back = jnp.concatenate([back_half[...], back_recv[...]], axis=0)
        emit(dot(place_buf[...], back, ((0,), (0,))))
        wait_all(ids_send, ids_out)
        wait_all(flux_send, flux_out)

    @pl.when(section == 1)
    def _():
        upper = me >= half

        @pl.when(upper)
        def _():
            wait_all(reply_recv.at[pl.ds(0, half - 1)], reply_in)

        @pl.when(jnp.logical_not(upper))
        def _():
            wait_all(reply_recv, reply_in)

        back_terms(half_slots)
        back_copy = pltpu.make_async_remote_copy(
            src_ref=back_half,
            dst_ref=back_recv,
            send_sem=back_out,
            recv_sem=back_in,
            device_id=(other, me),
            device_id_type=MESH,
        )
        back_copy.start()
        wait_all(flux_recv, flux_in)
        emit(dot(place_buf[...], flux_recv[...].reshape(slots, MXU), ((0,), (0,))))
        back_copy.wait_send()

        @pl.when(upper)
        def _():
            wait_all(reply_send.at[pl.ds(0, tiles - 1)], reply_out)

        @pl.when(jnp.logical_not(upper))
        def _():
            wait_all(reply_send, reply_out)


def layout(levels, cells):
    rows = round_up(levels, 16)
    full = round_up(rows, MXU)
    group = full // rows
    lanes = next(lanes for lanes in (512, 256, 128) if cells % (4 * group * lanes) == 0)
    return rows, full, group, lanes, 2


def exchange(surface, weights, pair_atmos, pair_ocean, list_len, owned, state, coef, operators):
    tiles, cap = pair_atmos.shape
    pairs = surface.shape[1]
    slots = tiles * cap
    half = tiles // 2
    _, levels, cells = state.shape
    steps = operators.shape[0]
    rows, full, group, lanes, units = layout(levels, cells)
    block = group * lanes * units
    early = cells // block // 2
    in_vmem = pl.BlockSpec(memory_space=pltpu.VMEM)
    in_place = pl.BlockSpec(memory_space=pl.ANY)
    return pl.pallas_call(
        functools.partial(exchange_kernel, tiles, cap, levels, rows, group, lanes, units),
        out_shape=(
            jax.ShapeDtypeStruct((pairs, NF, 2 * BLK), F32),
            jax.ShapeDtypeStruct((early, units * lanes, full), BF16),
        ),
        in_specs=[in_vmem] * 6 + [in_place] * 2 + [in_vmem],
        out_specs=(in_vmem, in_vmem),
        scratch_shapes=[
            pltpu.VMEM((tiles, 8, 128), jnp.int32),
            pltpu.VMEM((tiles, 8, 128), jnp.int32),
            pltpu.VMEM((tiles, cap, MXU), BF16),
            pltpu.VMEM((tiles, cap, MXU), BF16),
            pltpu.VMEM((tiles, cap, MXU), BF16),
            pltpu.VMEM((half, cap, MXU), BF16),
            pltpu.VMEM((half * cap, MXU), BF16),
            pltpu.VMEM((half * cap, MXU), BF16),
            pltpu.VMEM((slots, 2 * pairs), BF16),
            pltpu.VMEM((NF, half * cap, MXU), F32),
            pltpu.VMEM((NF, slots, MXU), F32),
            pltpu.VMEM((NF * half * cap, BLK), F32),
            pltpu.VMEM((early, levels, block), BF16),
            pltpu.VMEM((early, levels, block), BF16),
            pltpu.VMEM((steps, full, full), BF16),
            pltpu.SemaphoreType.DMA((8,)),
            pltpu.SemaphoreType.DMA((2, early)),
        ],
        compiler_params=pltpu.CompilerParams(
            collective_id=0, has_side_effects=True, vmem_limit_bytes=56 * 1024 * 1024
        ),
        name="exchange",
    )(surface, weights, pair_atmos, pair_ocean, list_len, owned, state, coef, operators)


def sweep_kernel(
    levels, rows, group, lanes, units, early,
    state_ref, coef_ref, ops_ref, write_ref, forcing_ref, swept_ref, out_ref, big, write_big,
):
    index = pl.program_id(0)
    full = big.shape[1]
    depth = write_big.shape[0]
    strip = 4 * NF

    @pl.when(index == 0)
    def _():
        build_operators(levels, rows, group, ops_ref, big)
        write = write_ref[:, 0:levels]
        high = write.astype(BF16).astype(F32)
        parts = jnp.concatenate([high, high, write - high, jnp.zeros_like(write)], axis=0).astype(BF16)
        target = iota((levels, full), 1)
        tiler = one_hot((lax.rem(target, rows) == iota((levels, full), 0)) & (target < group * rows))
        tiled = dot(parts, tiler)
        lane = iota((strip, full), 1)
        write_big[...] = jnp.zeros_like(write_big)
        for part in range(group):
            inside = (lane >= part * rows) & (lane < (part + 1) * rows)
            write_big[part * strip : (part + 1) * strip, :] = jnp.where(inside, tiled, 0.0).astype(BF16)

    def columns(unit, part):
        return pl.ds((unit * group + part) * lanes, lanes)

    def finish(swept, unit):
        pieces = []
        for part in range(group):
            first = (unit * group + part) * lanes // (2 * BLK)
            forcing = jnp.concatenate([forcing_ref[first + r] for r in range(lanes // (2 * BLK))], axis=1)
            high = forcing.astype(BF16).astype(F32)
            pieces.append(jnp.concatenate([high, forcing - high, high, jnp.zeros_like(high)], axis=0).astype(BF16))
        added = dot(stack_columns(pieces, depth), write_big[...])
        result = (swept.astype(F32) + added).astype(BF16).T
        for part in range(group):
            out_ref[0, :, columns(unit, part)] = result[part * rows : (part + 1) * rows]

    @pl.when(index < early)
    def _():
        half = units // 2
        for unit in range(units):
            first = unit % half * lanes
            finish(swept_ref[unit // half, first : first + lanes, :], unit)

    @pl.when(index >= early)
    def _():
        valid = iota((rows, lanes), 0) < levels

        def stacked(ref, unit):
            pieces = [
                jnp.where(valid, ref[0, :, columns(unit, part)].astype(F32), 0.0).astype(BF16)
                for part in range(group)
            ]
            return stack_columns(pieces, full)

        current = [stacked(state_ref, unit) for unit in range(units)]
        factors = [stacked(coef_ref, unit).astype(F32) for unit in range(units)]
        current = all_steps(current, factors, big)
        for unit in range(units):
            finish(current[unit], unit)


def sweep(state, coef, operators, surf_write, forcing, swept):
    _, levels, cells = state.shape
    steps = operators.shape[0]
    rows, full, group, lanes, units = layout(levels, cells)
    units = 2 * units
    block = group * lanes * units
    early = swept.shape[0] // 2
    wide = pl.BlockSpec((1, rows, block), lambda i: (0, 0, jnp.maximum(i, early)))
    return pl.pallas_call(
        functools.partial(sweep_kernel, levels, rows, group, lanes, units, early),
        out_shape=jax.ShapeDtypeStruct(state.shape, BF16),
        grid=(cells // block,),
        in_specs=[
            wide,
            wide,
            pl.BlockSpec(operators.shape, lambda i: (0, 0, 0)),
            pl.BlockSpec((NF, round_up(rows, 128)), lambda i: (0, 0)),
            pl.BlockSpec((block // (2 * BLK), NF, 2 * BLK), lambda i: (i, 0, 0)),
            pl.BlockSpec((2, units // 2 * lanes, full), lambda i: (jnp.minimum(i, early - 1), 0, 0)),
        ],
        out_specs=pl.BlockSpec((1, rows, block), lambda i: (0, 0, i)),
        scratch_shapes=[
            pltpu.VMEM((steps, full, full), BF16),
            pltpu.VMEM((round_up(4 * NF * group, 128), full), BF16),
        ],
        compiler_params=pltpu.CompilerParams(
            dimension_semantics=("arbitrary",), vmem_limit_bytes=56 * 1024 * 1024
        ),
        name="sweep",
    )(state, coef, operators, surf_write[0].T, forcing, swept)


def body(
    adjoint_state,
    tangent_coef,
    column_ops,
    surf_read,
    surf_write,
    remap_weights,
    pair_atmos,
    pair_ocean,
    list_len,
    ocean_owned,
):
    tiles, cap = pair_atmos.shape[1:]
    pairs = ocean_owned.shape[1] // 2
    surface = jnp.dot(surf_read[0], adjoint_state[0], preferred_element_type=F32).astype(BF16)
    owned = jnp.swapaxes(ocean_owned.reshape(pairs, 2), 0, 1).reshape(1, 2 * pairs)
    forcing, swept = exchange(
        surface.reshape(NF, pairs, 2 * BLK),
        remap_weights.reshape(tiles * cap, BLK * BLK),
        pair_atmos[0],
        pair_ocean[0],
        list_len,
        owned,
        adjoint_state,
        tangent_coef,
        column_ops[0],
    )
    return sweep(adjoint_state, tangent_coef, column_ops[0], surf_write, forcing, swept)


def solution(mesh):
    in_specs = (
        P("sec", None, "tile"),
        P("sec", None, "tile"),
        P("sec", None, None, None),
        P("sec", None, None),
        P("sec", None, None),
        P("tile", None, None, None),
        P("tile", None, None),
        P("tile", None, None),
        P("tile", None),
        P("tile", None),
    )
    out_specs = P("sec", None, "tile")
    return jax.shard_map(body, mesh=mesh, in_specs=in_specs, out_specs=out_specs, check_vma=False)
```

```python
import functools

import jax
import jax.numpy as jnp
from jax import lax
from jax.experimental import pallas as pl
from jax.experimental.pallas import tpu as pltpu
from jax.sharding import PartitionSpec as P

NF = 4
BLK = 64
MXU = 256
MESH = pl.DeviceIdType.MESH
F32 = jnp.float32
BF16 = jnp.bfloat16


def round_up(value, unit):
    return -(-value // unit) * unit


def iota(shape, axis):
    return lax.broadcasted_iota(jnp.int32, shape, axis)


def dot(left, right, contract=((1,), (0,))):
    return lax.dot_general(left, right, (contract, ((), ())), preferred_element_type=F32)


def one_hot(condition):
    return jnp.where(condition, 1.0, 0.0).astype(BF16)


def slot_column(rows, cap):
    spread = jnp.concatenate([jnp.broadcast_to(row, (cap, row.shape[1])) for row in rows], axis=0)
    chosen = iota(spread.shape, 1) == lax.rem(iota(spread.shape, 0), cap)
    return jnp.sum(jnp.where(chosen, spread.astype(F32), 0.0), axis=1, keepdims=True)


def build_operators(levels, rows, group, ops_ref, big):
    full = big.shape[1]
    lane = iota((rows, full), 1)
    target = iota((levels, full), 1)
    tiler = one_hot((lax.rem(target, rows) == iota((levels, full), 0)) & (target < group * rows))
    blank = jnp.zeros((rows - levels, levels), F32)
    steps = ops_ref.shape[0]
    pieces = []
    for step in range(steps):
        pieces.append(jnp.concatenate([ops_ref[step].astype(F32), blank], axis=0).astype(BF16))
    all_tiled = dot(jnp.concatenate(pieces, axis=0), tiler).astype(BF16)
    for step in range(steps):
        tiled = all_tiled[step * rows : (step + 1) * rows].astype(F32)
        for part in range(group):
            inside = (lane >= part * rows) & (lane < (part + 1) * rows)
            big[step, part * rows : (part + 1) * rows, :] = jnp.where(inside, tiled, 0.0).astype(BF16)
        if full > group * rows:
            big[step, group * rows :, :] = jnp.zeros((full - group * rows, full), BF16)


def stack_columns(pieces, full):
    stacked = sum(piece.shape[0] for piece in pieces)
    if full > stacked:
        pieces = pieces + [jnp.zeros((full - stacked, pieces[0].shape[1]), BF16)]
    return jnp.concatenate(pieces, axis=0).T


def all_steps(current, factors, big):
    for step in range(big.shape[0]):
        for unit in range(len(current)):
            current[unit] = (dot(current[unit], big[step]) * factors[unit]).astype(BF16)
    return current


def exchange_kernel(
    tiles, cap, levels, rows, group, lanes, units,
    surface_ref, weights_ref, atmos_ref, ocean_ref, len_ref, owned_ref, state_ref, coef_ref, ops_ref,
    out_ref, swept_ref,
    ids_send, ids_recv, flux_send, flux_recv, reply_send, reply_recv, back_half, back_recv, place_buf,
    expanded, summed, folded, state_buf, coef_buf, big, sems, load_sems,
):
    section = lax.axis_index("sec")
    me = lax.axis_index("tile")
    other = 1 - section
    slots = tiles * cap
    half = tiles // 2
    half_slots = half * cap
    pairs = surface_ref.shape[1]
    blocks = 2 * pairs
    wide = 2 * MXU
    chunks = weights_ref.shape[1] // wide
    per_chunk = wide // BLK
    ids_out, ids_in, flux_out, flux_in, reply_out, reply_in, back_out, back_in = [sems.at[i] for i in range(8)]

    def peer(i):
        return lax.rem(me + i, tiles)

    early = swept_ref.shape[0]
    block_cells = group * lanes * units
    full = big.shape[1]

    def load(source, target, kind, j):
        start = pl.multiple_of(j * block_cells, block_cells)
        return pltpu.make_async_copy(
            source.at[0, :, pl.ds(start, block_cells)], target.at[j], load_sems.at[kind, j]
        )

    for j in range(early):
        load(state_ref, state_buf, 0, j).start()
        load(coef_ref, coef_buf, 1, j).start()

    def sweep_blocks(first, last):
        @pl.loop(first, last)
        def _(j):
            load(state_ref, state_buf, 0, j).wait()
            load(coef_ref, coef_buf, 1, j).wait()

            def columns(unit, part):
                return pl.ds((unit * group + part) * lanes, lanes)

            def stacked(buffer, unit):
                pieces = []
                for part in range(group):
                    piece = buffer[j, :, columns(unit, part)].astype(F32)
                    blank = jnp.zeros((rows - levels, lanes), F32)
                    pieces.append(jnp.concatenate([piece, blank], axis=0).astype(BF16))
                return stack_columns(pieces, full)

            current = [stacked(state_buf, unit) for unit in range(units)]
            factors = [stacked(coef_buf, unit).astype(F32) for unit in range(units)]
            current = all_steps(current, factors, big)
            for unit in range(units):
                swept_ref[j, unit * lanes : (unit + 1) * lanes, :] = current[unit]

    barrier = pltpu.get_barrier_semaphore()

    @pl.loop(0, tiles)
    def _(i):
        pl.semaphore_signal(barrier, inc=1, device_id=(other, peer(i)), device_id_type=MESH)

    @pl.when(section == 1)
    def _():
        @pl.loop(1, tiles)
        def _(i):
            pl.semaphore_signal(barrier, inc=1, device_id=(section, peer(i)), device_id_type=MESH)

    def send(source, target, send_sem, recv_sem, first, to):
        @pl.loop(first, tiles)
        def _(i):
            pltpu.make_async_remote_copy(
                src_ref=source.at[peer(i)],
                dst_ref=target,
                send_sem=send_sem,
                recv_sem=recv_sem,
                device_id=(to, peer(i)),
                device_id_type=MESH,
            ).start()

    def wait_all(buffer, sem):
        pltpu.make_async_copy(buffer, buffer, sem).wait()

    def surface_rows():
        lower = [surface_ref[n, :, 0:BLK] for n in range(NF)]
        upper = [surface_ref[n, :, BLK : 2 * BLK] for n in range(NF)]
        return jnp.concatenate([jnp.concatenate(lower, axis=1), jnp.concatenate(upper, axis=1)], axis=0)

    def emit(forcing):
        for n in range(NF):
            lanes = slice(n * BLK, (n + 1) * BLK)
            out_ref[:, n, :] = jnp.concatenate([forcing[:pairs, lanes], forcing[pairs:, lanes]], axis=1)

    def weights_at(q, first, count):
        return weights_ref[first : first + count, pl.ds(pl.multiple_of(q * wide, wide), wide)].astype(F32)

    def back_terms(first):
        echoes = reply_recv[...].reshape(half_slots, MXU)
        for n in range(NF):
            repeat = one_hot(iota((MXU, MXU), 0) == n * BLK + lax.rem(iota((MXU, MXU), 1), BLK))
            expanded[n] = dot(echoes, repeat)
        folded[...] = jnp.zeros_like(folded)

        @pl.loop(0, chunks)
        def _(q):
            weights = weights_at(q, first, half_slots)
            gather = one_hot(iota((wide, BLK), 1) == q * per_chunk + iota((wide, BLK), 0) // BLK)
            products = []
            for n in range(NF):
                copies = jnp.concatenate([expanded[n], expanded[n]], axis=1)
                products.append((copies * weights).astype(BF16))
            folded[...] += dot(jnp.concatenate(products, axis=0), gather)

        fields = [folded[n * half_slots : (n + 1) * half_slots] for n in range(NF)]
        back_half[...] = jnp.concatenate(fields, axis=1).astype(BF16)

    build_operators(levels, rows, group, ops_ref, big)

    @pl.when(section == 0)
    def _():
        for d in range(tiles):
            ids_send[d, 0:1, 0:cap] = ocean_ref[d : d + 1, :]
        source = slot_column([atmos_ref[d : d + 1, :] for d in range(tiles)], cap)
        spread = jnp.broadcast_to(len_ref[...], (slots, tiles))
        owner = iota((slots, tiles), 1) == iota((slots, tiles), 0) // cap
        length = jnp.sum(jnp.where(owner, spread.astype(F32), 0.0), axis=1, keepdims=True)
        live = lax.rem(iota((slots, 1), 0), cap).astype(F32) < length
        lane = iota((slots, blocks), 1)
        block = 2 * lax.rem(lane, pairs) + lane // pairs
        place = one_hot((block.astype(F32) == source) & live)
        place_buf[...] = place
        picked = dot(place, surface_rows()).astype(BF16)
        fields = jnp.concatenate([picked[:, n * BLK : (n + 1) * BLK] for n in range(NF)], axis=0)
        summed[...] = jnp.zeros_like(summed)

        @pl.loop(0, chunks)
        def _(q):
            weights = weights_at(q, 0, slots)
            widen = one_hot(iota((BLK, wide), 0) == q * per_chunk + iota((BLK, wide), 1) // BLK)
            widened = dot(fields, widen)
            for n in range(NF):
                terms = widened[n * slots : (n + 1) * slots] * weights
                summed[n] += terms[:, :MXU] + terms[:, MXU:]

        flux = jnp.zeros((slots, MXU), F32)
        for n in range(NF):
            fold = one_hot(iota((MXU, MXU), 1) == n * BLK + lax.rem(iota((MXU, MXU), 0), BLK))
            flux += dot(summed[n].astype(BF16), fold)
        flux_send[...] = flux.astype(BF16).reshape(tiles, cap, MXU)

    middle = section * (2 * early // 3)
    sweep_blocks(0, middle)

    @pl.when(section == 0)
    def _():
        pl.semaphore_wait(barrier, tiles)
        send(ids_send, ids_recv.at[me], ids_out, ids_in, 0, 1)
        send(flux_send, flux_recv.at[me], flux_out, flux_in, 0, 1)

    @pl.when(section == 1)
    def _():
        pl.semaphore_wait(barrier, 2 * tiles - 1)
        surface = surface_rows()
        wait_all(ids_recv, ids_in)
        wanted = slot_column([ids_recv[t, 0:1, :] for t in range(tiles)], cap)
        place = one_hot(owned_ref[...].astype(F32) == wanted)
        place_buf[...] = place
        reply_send[...] = dot(place, surface).astype(BF16).reshape(tiles, cap, MXU)

        @pl.when(me >= half)
        def _():
            send(reply_send, reply_recv.at[me - half], reply_out, reply_in, 1, 1)
            reply_recv[me - half] = reply_send[me]

        @pl.when(me < half)
        def _():
            send(reply_send, reply_recv.at[me], reply_out, reply_in, 0, 0)

    sweep_blocks(middle, early)

    @pl.when(section == 0)
    def _():
        wait_all(reply_recv, reply_in)
        back_terms(0)
        wait_all(back_recv, back_in)
        back = jnp.concatenate([back_half[...], back_recv[...]], axis=0)
        emit(dot(place_buf[...], back, ((0,), (0,))))
        wait_all(ids_send, ids_out)
        wait_all(flux_send, flux_out)

    @pl.when(section == 1)
    def _():
        upper = me >= half

        @pl.when(upper)
        def _():
            wait_all(reply_recv.at[pl.ds(0, half - 1)], reply_in)

        @pl.when(jnp.logical_not(upper))
        def _():
            wait_all(reply_recv, reply_in)

        back_terms(half_slots)
        back_copy = pltpu.make_async_remote_copy(
            src_ref=back_half,
            dst_ref=back_recv,
            send_sem=back_out,
            recv_sem=back_in,
            device_id=(other, me),
            device_id_type=MESH,
        )
        back_copy.start()
        wait_all(flux_recv, flux_in)
        emit(dot(place_buf[...], flux_recv[...].reshape(slots, MXU), ((0,), (0,))))
        back_copy.wait_send()

        @pl.when(upper)
        def _():
            wait_all(reply_send.at[pl.ds(0, tiles - 1)], reply_out)

        @pl.when(jnp.logical_not(upper))
        def _():
            wait_all(reply_send, reply_out)


def layout(levels, cells):
    rows = round_up(levels, 16)
    full = round_up(rows, MXU)
    group = full // rows
    lanes = next(lanes for lanes in (512, 256, 128) if cells % (4 * group * lanes) == 0)
    return rows, full, group, lanes, 2


def exchange(surface, weights, pair_atmos, pair_ocean, list_len, owned, state, coef, operators):
    tiles, cap = pair_atmos.shape
    pairs = surface.shape[1]
    slots = tiles * cap
    half = tiles // 2
    _, levels, cells = state.shape
    steps = operators.shape[0]
    rows, full, group, lanes, units = layout(levels, cells)
    block = group * lanes * units
    early = cells // block // 2
    in_vmem = pl.BlockSpec(memory_space=pltpu.VMEM)
    in_place = pl.BlockSpec(memory_space=pl.ANY)
    return pl.pallas_call(
        functools.partial(exchange_kernel, tiles, cap, levels, rows, group, lanes, units),
        out_shape=(
            jax.ShapeDtypeStruct((pairs, NF, 2 * BLK), F32),
            jax.ShapeDtypeStruct((early, units * lanes, full), BF16),
        ),
        in_specs=[in_vmem] * 6 + [in_place] * 2 + [in_vmem],
        out_specs=(in_vmem, in_vmem),
        scratch_shapes=[
            pltpu.VMEM((tiles, 8, 128), jnp.int32),
            pltpu.VMEM((tiles, 8, 128), jnp.int32),
            pltpu.VMEM((tiles, cap, MXU), BF16),
            pltpu.VMEM((tiles, cap, MXU), BF16),
            pltpu.VMEM((tiles, cap, MXU), BF16),
            pltpu.VMEM((half, cap, MXU), BF16),
            pltpu.VMEM((half * cap, MXU), BF16),
            pltpu.VMEM((half * cap, MXU), BF16),
            pltpu.VMEM((slots, 2 * pairs), BF16),
            pltpu.VMEM((NF, half * cap, MXU), F32),
            pltpu.VMEM((NF, slots, MXU), F32),
            pltpu.VMEM((NF * half * cap, BLK), F32),
            pltpu.VMEM((early, levels, block), BF16),
            pltpu.VMEM((early, levels, block), BF16),
            pltpu.VMEM((steps, full, full), BF16),
            pltpu.SemaphoreType.DMA((8,)),
            pltpu.SemaphoreType.DMA((2, early)),
        ],
        compiler_params=pltpu.CompilerParams(
            collective_id=0, has_side_effects=True, vmem_limit_bytes=56 * 1024 * 1024
        ),
        name="exchange",
    )(surface, weights, pair_atmos, pair_ocean, list_len, owned, state, coef, operators)


def sweep_kernel(
    levels, rows, group, lanes, units, early,
    state_ref, coef_ref, ops_ref, write_ref, forcing_ref, swept_ref, out_ref, big, write_big,
):
    index = pl.program_id(0)
    full = big.shape[1]
    depth = write_big.shape[0]
    strip = 4 * NF

    @pl.when(index == 0)
    def _():
        build_operators(levels, rows, group, ops_ref, big)
        write = write_ref[:, 0:levels]
        high = write.astype(BF16).astype(F32)
        parts = jnp.concatenate([high, high, write - high, jnp.zeros_like(write)], axis=0).astype(BF16)
        target = iota((levels, full), 1)
        tiler = one_hot((lax.rem(target, rows) == iota((levels, full), 0)) & (target < group * rows))
        tiled = dot(parts, tiler)
        lane = iota((strip, full), 1)
        write_big[...] = jnp.zeros_like(write_big)
        for part in range(group):
            inside = (lane >= part * rows) & (lane < (part + 1) * rows)
            write_big[part * strip : (part + 1) * strip, :] = jnp.where(inside, tiled, 0.0).astype(BF16)

    def columns(unit, part):
        return pl.ds((unit * group + part) * lanes, lanes)

    def finish(swept, unit):
        pieces = []
        for part in range(group):
            first = (unit * group + part) * lanes // (2 * BLK)
            forcing = jnp.concatenate([forcing_ref[first + r] for r in range(lanes // (2 * BLK))], axis=1)
            high = forcing.astype(BF16).astype(F32)
            pieces.append(jnp.concatenate([high, forcing - high, high, jnp.zeros_like(high)], axis=0).astype(BF16))
        added = dot(stack_columns(pieces, depth), write_big[...])
        result = (swept.astype(F32) + added).astype(BF16).T
        for part in range(group):
            out_ref[0, :, columns(unit, part)] = result[part * rows : (part + 1) * rows]

    @pl.when(index < early)
    def _():
        half = units // 2
        for unit in range(units):
            first = unit % half * lanes
            finish(swept_ref[unit // half, first : first + lanes, :], unit)

    @pl.when(index >= early)
    def _():
        valid = iota((rows, lanes), 0) < levels

        def stacked(ref, unit):
            pieces = [
                jnp.where(valid, ref[0, :, columns(unit, part)].astype(F32), 0.0).astype(BF16)
                for part in range(group)
            ]
            return stack_columns(pieces, full)

        current = [stacked(state_ref, unit) for unit in range(units)]
        factors = [stacked(coef_ref, unit).astype(F32) for unit in range(units)]
        current = all_steps(current, factors, big)
        for unit in range(units):
            finish(current[unit], unit)


def sweep(state, coef, operators, surf_write, forcing, swept):
    _, levels, cells = state.shape
    steps = operators.shape[0]
    rows, full, group, lanes, units = layout(levels, cells)
    units = 2 * units
    block = group * lanes * units
    early = swept.shape[0] // 2
    wide = pl.BlockSpec((1, rows, block), lambda i: (0, 0, jnp.maximum(i, early)))
    return pl.pallas_call(
        functools.partial(sweep_kernel, levels, rows, group, lanes, units, early),
        out_shape=jax.ShapeDtypeStruct(state.shape, BF16),
        grid=(cells // block,),
        in_specs=[
            wide,
            wide,
            pl.BlockSpec(operators.shape, lambda i: (0, 0, 0)),
            pl.BlockSpec((NF, round_up(rows, 128)), lambda i: (0, 0)),
            pl.BlockSpec((block // (2 * BLK), NF, 2 * BLK), lambda i: (i, 0, 0)),
            pl.BlockSpec((2, units // 2 * lanes, full), lambda i: (jnp.minimum(i, early - 1), 0, 0)),
        ],
        out_specs=pl.BlockSpec((1, rows, block), lambda i: (0, 0, i)),
        scratch_shapes=[
            pltpu.VMEM((steps, full, full), BF16),
            pltpu.VMEM((round_up(4 * NF * group, 128), full), BF16),
        ],
        compiler_params=pltpu.CompilerParams(
            dimension_semantics=("arbitrary",), vmem_limit_bytes=56 * 1024 * 1024
        ),
        name="sweep",
    )(state, coef, operators, surf_write[0].T, forcing, swept)


def body(
    adjoint_state,
    tangent_coef,
    column_ops,
    surf_read,
    surf_write,
    remap_weights,
    pair_atmos,
    pair_ocean,
    list_len,
    ocean_owned,
):
    tiles, cap = pair_atmos.shape[1:]
    pairs = ocean_owned.shape[1] // 2
    surface = jnp.dot(surf_read[0], adjoint_state[0], preferred_element_type=F32).astype(BF16)
    owned = jnp.swapaxes(ocean_owned.reshape(pairs, 2), 0, 1).reshape(1, 2 * pairs)
    forcing, swept = exchange(
        surface.reshape(NF, pairs, 2 * BLK),
        remap_weights.reshape(tiles * cap, BLK * BLK),
        pair_atmos[0],
        pair_ocean[0],
        list_len,
        owned,
        adjoint_state,
        tangent_coef,
        column_ops[0],
    )
    return sweep(adjoint_state, tangent_coef, column_ops[0], surf_write, forcing, swept)


def solution(mesh):
    in_specs = (
        P("sec", None, "tile"),
        P("sec", None, "tile"),
        P("sec", None, None, None),
        P("sec", None, None),
        P("sec", None, None),
        P("tile", None, None, None),
        P("tile", None, None),
        P("tile", None, None),
        P("tile", None),
        P("tile", None),
    )
    out_specs = P("sec", None, "tile")
    return jax.shard_map(body, mesh=mesh, in_specs=in_specs, out_specs=out_specs, check_vma=False)
```
